32 devices in a mesh: chan: 32 (over z, y, x, core), tile: 1.
Axes of the slice: x: 2, y: 2, z: 4, core: 2. Of those that a mesh axis runs over, the one named last changes fastest.
Arguments:
- voltage: bfloat16 [1024, 131072], P('tile', 'chan'), may hold values from -6 to 6
- tap_weights: float32 [4, 1024], replicated, may hold values from -3 to 3
Outputs:
- visibility: float32 [512, 1024, 1024], P('chan', 'tile')
The draws below stay inside these ranges and needn't reach their ends.
All inputs are finite; a program needn't handle non-finite values.
Results may differ from the reference program's by a relative error of at most 0.0047.
Values may be sent and summed in bfloat16 or wider, within the bound.
No kernel may reach another device: no remote copies, remote signals or barrier semaphores. Data moves between devices by JAX's collectives and lax.ppermute only.
A program may use at most 384 MiB of HBM per device.

```python
import math
import jax
import jax.numpy as jnp
from jax import lax

NIN = 1024
CHAN = 512
TAPS = 4
FRAME = 1024
SPEC = 128


def level_of(own_key, dims, shards, least, high):
    def one(axis_at, blocks):
        steps = jax.random.uniform(jax.random.fold_in(jax.random.fold_in(own_key, 6), axis_at), (blocks,), jnp.float32, least / len(shards), high / len(shards))
        return jnp.repeat(jnp.exp(steps), dims[axis_at] // blocks).reshape((-1,) + (1,) * (len(dims) - axis_at - 1))

    gain = one(*shards[0])
    for cut in shards[1:]:
        gain = gain * one(*cut)
    return gain


def bell_draw(rng, extent, spread, bound, split=(), held_as=jnp.bfloat16):
    level = level_of(rng, extent, split, -0.22, 0.18) if split else 1.0
    values = jax.random.normal(rng, extent, jnp.float32) * spread * level
    return jnp.minimum(jnp.maximum(values, -bound), bound).astype(held_as)


def setup_inputs(seed: int = 0) -> dict:
    seeds = jax.random.split(jax.random.key(seed), 3)
    return {
        "voltage": bell_draw(seeds[0], (NIN, SPEC * FRAME), 1.0, 6.0, ((1, 32),)),
        "tap_weights": bell_draw(seeds[1], (TAPS, FRAME), TAPS ** -0.5, 3.0, (), jnp.float32),
    }


def transform_table(frame_len, channels):
    sample_index = lax.iota(jnp.int32, frame_len)
    channel_index = lax.iota(jnp.int32, channels)
    phase_index = channel_index[:, None] * sample_index[None, :] % frame_len
    angle_value = phase_index.astype(jnp.float32) * (2.0 * math.pi / frame_len)
    norm_factor = 1.0 / math.sqrt(frame_len)
    cos_part = jnp.cos(angle_value) * norm_factor
    sin_part = -jnp.sin(angle_value) * norm_factor
    return jnp.concatenate([cos_part, sin_part], 0).astype(jnp.bfloat16)

def reference(voltage, tap_weights):
    frame_len = 2 * CHAN
    inputs_all = voltage.shape[0]
    spectra_count = voltage.shape[1] // frame_len
    block_size = min(inputs_all, 64)
    block_count = inputs_all // block_size
    dft_table = transform_table(frame_len, CHAN).astype(jnp.float32)

    def filter_block(voltage_block):
        frames = voltage_block.reshape(block_size, spectra_count, frame_len).astype(jnp.float32)
        padded = jnp.concatenate([jnp.zeros((block_size, TAPS - 1, frame_len), jnp.float32), frames], 1)
        filtered = jnp.zeros((block_size, spectra_count, frame_len), jnp.float32)
        for tap_index in range(TAPS):
            shifted = padded[:, TAPS - 1 - tap_index:TAPS - 1 - tap_index + spectra_count, :]
            filtered = filtered + tap_weights[tap_index][None, None, :] * shifted
        filtered = filtered.astype(jnp.bfloat16).astype(jnp.float32)
        spectrum = jnp.dot(dft_table, filtered.reshape(block_size * spectra_count, frame_len).T, precision=lax.Precision.HIGHEST)
        return spectrum.astype(jnp.bfloat16)
    blocks = lax.map(filter_block, voltage.reshape(block_count, block_size, -1))
    blocks = blocks.reshape(block_count, 2, CHAN, block_size, spectra_count)
    spectra = jnp.transpose(blocks, (2, 1, 0, 3, 4)).reshape(CHAN, 2, inputs_all, spectra_count)
    row_index = lax.iota(jnp.int32, inputs_all)[:, None]
    col_index = lax.iota(jnp.int32, inputs_all)[None, :]

    def channel_products(channel_block):
        real_part = channel_block[0].astype(jnp.float32)
        imag_part = channel_block[1].astype(jnp.float32)
        stacked_re = jnp.concatenate([real_part, imag_part], 1)
        stacked_im = jnp.concatenate([imag_part, -real_part], 1)
        vis_re = jnp.dot(stacked_re, stacked_re.T, precision=lax.Precision.HIGHEST) / spectra_count
        vis_im = jnp.dot(stacked_im, stacked_re.T, precision=lax.Precision.HIGHEST) / spectra_count
        return jnp.where(col_index >= row_index, vis_re, vis_im)
    return lax.map(channel_products, spectra)
```

```python
import functools
import math

import jax
import jax.numpy as jnp
import ml_dtypes
import numpy as np
from jax import lax
from jax.experimental import pallas as pl
from jax.experimental.pallas import tpu as pltpu
from jax.sharding import PartitionSpec as P

CHAN = 512
TAPS = 4
VMEM_LIMIT = 56 * 1024 * 1024
FILTER_ROWS = 32
LANES = 128


def passed_along(block, axis, distance):
    devices = range(lax.axis_size(axis))
    route = [(i - distance, i) for i in devices if i - distance in devices]
    return lax.ppermute(block, axis, route)


def transform_table(frame_len, channels):
    phase = np.arange(channels)[:, None] * np.arange(frame_len)[None, :] % frame_len
    angle = phase * (2.0 * math.pi / frame_len)
    rows = np.stack([np.cos(angle), -np.sin(angle)], 1) / math.sqrt(frame_len)
    return rows.reshape(2 * channels, frame_len).astype(np.float32).astype(ml_dtypes.bfloat16)


def cost(flops, moved):
    return pl.CostEstimate(flops=flops, bytes_accessed=moved, transcendentals=0)


def filter_transform_kernel(frame_of, spectra, dests, splits, sources, *refs):
    voltage_refs = refs[:sources]
    weights_ref, table_ref = refs[sources : sources + 2]
    out_refs = refs[sources + 2 : -1]
    filtered_ref = refs[-1]
    rows, frame_len = filtered_ref.shape[1:]
    needed = sorted({s - k for s in spectra for k in range(TAPS)})

    for lane in range(0, frame_len, LANES):
        weights = [
            jnp.broadcast_to(weights_ref[k : k + 1, lane : lane + LANES], (FILTER_ROWS, LANES))
            for k in range(TAPS)
        ]

        def body(step, carry, lane=lane, weights=weights):
            at = pl.ds(pl.multiple_of(step * FILTER_ROWS, FILTER_ROWS), FILTER_ROWS)
            frames = {}
            for f in needed:
                source, place = frame_of[f]
                start = place * frame_len + lane
                frames[f] = voltage_refs[source][at, start : start + LANES].astype(jnp.float32)
            for slot, s in enumerate(spectra):
                total = weights[0] * frames[s]
                for k in range(1, TAPS):
                    total = total + weights[k] * frames[s - k]
                filtered_ref[slot, at, lane : lane + LANES] = total.astype(jnp.bfloat16)
            return carry

        lax.fori_loop(0, rows // FILTER_ROWS, body, 0, unroll=2)

    per_dest = table_ref.shape[0] // dests
    dest_block = max(1, 256 // per_dest)
    for slot in range(len(spectra)):
        filtered = filtered_ref[slot]
        for first in range(0, dests, dest_block):
            part = table_ref[first * per_dest : (first + dest_block) * per_dest, :]
            spectrum = lax.dot_general(
                part, filtered, (((1,), (1,)), ((), ())), preferred_element_type=jnp.float32
            )
            spectrum = spectrum.astype(jnp.bfloat16).reshape(dest_block, per_dest, rows)
            begin = 0
            for out_ref, width in zip(out_refs, splits):
                out_ref[first : first + dest_block, slot] = spectrum[:, begin : begin + width, :]
                begin += width


def filter_transform(arrays, frame_of, spectra, weights, table, dests, splits, rows, first_row=0):
    frame_len = table.shape[1]
    block = min(256, rows)
    per_dest = table.shape[0] // dests
    count = len(spectra)
    begin = first_row // block
    widths = [a.shape[1] for a in arrays]
    begins = [begin if a.shape[0] > rows else 0 for a in arrays]
    in_specs = [
        pl.BlockSpec((block, w), functools.partial(lambda b, i: (i + b, 0), b))
        for w, b in zip(widths, begins)
    ]
    in_specs += [
        pl.BlockSpec(weights.shape, lambda i: (0, 0)),
        pl.BlockSpec(table.shape, lambda i: (0, 0)),
    ]
    return pl.pallas_call(
        functools.partial(
            filter_transform_kernel, frame_of, tuple(spectra), dests, tuple(splits), len(arrays)
        ),
        grid=(rows // block,),
        in_specs=in_specs,
        out_specs=[pl.BlockSpec((dests, count, w, block), lambda i: (0, 0, 0, i)) for w in splits],
        out_shape=[
            jax.ShapeDtypeStruct((dests, count, w, rows), jnp.bfloat16) for w in splits
        ],
        scratch_shapes=[pltpu.VMEM((count, block, frame_len), jnp.bfloat16)],
        compiler_params=pltpu.CompilerParams(vmem_limit_bytes=VMEM_LIMIT),
        cost_estimate=cost(
            2 * table.size * rows * count, 2 * (sum(widths) * rows + table.size * (1 + count))
        ),
        name="filter_transform",
    )(*arrays, weights, table)


def regroup_kernel(sources, *refs):
    spectra_refs = refs[:sources]
    wide_ref, tall_ref, scratch = refs[sources:]
    rows = spectra_refs[0].shape[2]
    at = 0
    for ref in spectra_refs:
        devices, count, _, lanes = ref.shape
        for d in range(devices):
            block = ref[d].reshape(count * rows, lanes).astype(jnp.float32)
            for tile in range(lanes // LANES):
                scratch[tile, at : at + count * rows, :] = block[:, tile * LANES : (tile + 1) * LANES]
            at += count * rows
    depth = at // rows
    for channel in range(rows // 2):
        for part in range(2):
            deep = slice(part * depth, (part + 1) * depth)
            for tile in range(scratch.shape[0]):
                across = slice(tile * LANES, (tile + 1) * LANES)
                values = scratch[tile, pl.ds(2 * channel + part, depth, stride=rows), :]
                wide_ref[channel, deep, across] = values.astype(jnp.bfloat16)
                tall_ref[channel, across, deep] = values.T.astype(jnp.bfloat16)


def regroup(arrays, pieces, rows, inputs):
    block = min(256, inputs)
    depth = sum(a.shape[0] * a.shape[1] for a in arrays)
    channels = rows // 2
    in_specs = [
        pl.BlockSpec(
            (a.shape[0], a.shape[1], rows, block),
            functools.partial(lambda p, i: (0, 0, p, i), p),
        )
        for a, p in zip(arrays, pieces)
    ]
    return pl.pallas_call(
        functools.partial(regroup_kernel, len(arrays)),
        grid=(inputs // block,),
        in_specs=in_specs,
        out_specs=[
            pl.BlockSpec((channels, 2 * depth, block), lambda i: (0, 0, i)),
            pl.BlockSpec((channels, block, 2 * depth), lambda i: (0, i, 0)),
        ],
        out_shape=[
            jax.ShapeDtypeStruct((channels, 2 * depth, inputs), jnp.bfloat16),
            jax.ShapeDtypeStruct((channels, inputs, 2 * depth), jnp.bfloat16),
        ],
        scratch_shapes=[pltpu.VMEM((block // LANES, depth * rows, LANES), jnp.float32)],
        compiler_params=pltpu.CompilerParams(vmem_limit_bytes=VMEM_LIMIT),
        cost_estimate=cost(0, 6 * depth * rows * inputs),
        name="regroup",
    )(*arrays)


def correlate_kernel(scale, *refs):
    wide_ref, tall_ref, out_ref = refs[0], refs[1], refs[-1]
    depth, inputs = wide_ref.shape[1:]
    half = depth // 2
    block = min(256, inputs)
    wide = wide_ref[0]
    row_index = lax.broadcasted_iota(jnp.int32, (block, block), 0)
    col_index = lax.broadcasted_iota(jnp.int32, (block, block), 1)
    upper = col_index >= row_index
    for first in range(0, inputs, block):
        re_rows = tall_ref[0, first : first + block, :]
        im_rows = jnp.concatenate([re_rows[:, half:], -re_rows[:, :half]], 1)
        end = first + block
        im = jnp.dot(im_rows, wide[:, :end], preferred_element_type=jnp.float32) * scale
        re = jnp.dot(re_rows, wide[:, first:], preferred_element_type=jnp.float32) * scale
        if first:
            out_ref[0, first:end, :first] = im[:, :first]
        out_ref[0, first:end, first:end] = jnp.where(upper, re[:, :block], im[:, first:])
        if end < inputs:
            out_ref[0, first:end, end:] = re[:, block:]


def correlate(wide, tall, total_channels, first_channel, spectra_count, out=None):
    channels, depth, inputs = wide.shape
    in_specs = [
        pl.BlockSpec((1, depth, inputs), lambda c: (c, 0, 0)),
        pl.BlockSpec((1, inputs, depth), lambda c: (c, 0, 0)),
    ]
    args, aliases = [wide, tall], {}
    if out is not None:
        in_specs.append(pl.BlockSpec(memory_space=pl.ANY))
        args.append(out)
        aliases = {2: 0}
    return pl.pallas_call(
        functools.partial(correlate_kernel, 1.0 / spectra_count),
        grid=(channels,),
        in_specs=in_specs,
        out_specs=pl.BlockSpec((1, inputs, inputs), lambda c: (c + first_channel, 0, 0)),
        out_shape=jax.ShapeDtypeStruct((total_channels, inputs, inputs), jnp.float32),
        input_output_aliases=aliases,
        compiler_params=pltpu.CompilerParams(vmem_limit_bytes=VMEM_LIMIT),
        cost_estimate=cost(
            2 * channels * depth * inputs * inputs, channels * inputs * (4 * depth + 4 * inputs)
        ),
        name="correlate",
    )(*args)


def per_device(voltage, tap_weights):
    frame_len = 2 * CHAN
    inputs, samples = voltage.shape
    spec_local = samples // frame_len
    devices = lax.axis_size("chan")
    channels = CHAN // devices
    table = jnp.asarray(transform_table(frame_len, CHAN))
    past = TAPS - 1
    earlier = passed_along(voltage[:, samples - past * frame_len :], "chan", 1)
    frame_of = {f: (1, f) for f in range(spec_local)}
    frame_of.update({-1 - k: (0, past - 1 - k) for k in range(past)})
    splits = [channels, channels]
    blocks = filter_transform(
        [earlier, voltage], frame_of, range(spec_local), tap_weights, table, devices, splits, inputs
    )
    result = None
    for piece, block in enumerate(blocks):
        turned = lax.all_to_all(block, "chan", split_axis=0, concat_axis=0, tiled=True)
        wide, tall = regroup([turned], [0], channels, inputs)
        result = correlate(
            wide, tall, channels, piece * channels // 2, devices * spec_local, result
        )
    return result


def stack_operands(turned):
    stacked_re = jnp.concatenate([turned[0], turned[1]], -1)
    stacked_im = jnp.concatenate([turned[1], -turned[0]], -1)
    return jnp.stack([stacked_re, stacked_im], 0)


def pair_products(left_rows, right_cols):
    return jnp.einsum("pcik,cjk->pcij", left_rows, right_cols, preferred_element_type=jnp.float32)


def per_device_tiled(voltage, tap_weights):
    frame_len = 2 * CHAN
    local_inputs, samples = voltage.shape
    spec_local = samples // frame_len
    history_tail = voltage[:, samples - (TAPS - 1) * frame_len :]
    earlier = passed_along(history_tail, "chan", 1)
    extended = jnp.concatenate([earlier, voltage], 1).reshape(
        local_inputs, spec_local + TAPS - 1, frame_len
    )
    filtered = jnp.zeros((local_inputs, spec_local, frame_len), jnp.float32)
    for tap_index in range(TAPS):
        shifted = extended[:, TAPS - 1 - tap_index : TAPS - 1 - tap_index + spec_local, :]
        filtered = filtered + tap_weights[tap_index][None, None, :] * shifted.astype(jnp.float32)
    filtered = filtered.astype(jnp.bfloat16).reshape(local_inputs * spec_local, frame_len)
    dft_table = jnp.asarray(transform_table(frame_len, CHAN)).reshape(CHAN, 2, frame_len)
    dft_table = dft_table.swapaxes(0, 1).reshape(2 * CHAN, frame_len)
    spectra = lax.dot_general(
        dft_table, filtered, (((1,), (1,)), ((), ())), preferred_element_type=jnp.float32
    )
    spectra = spectra.astype(jnp.bfloat16).reshape(2, CHAN, local_inputs, spec_local)
    turned = lax.all_to_all(
        lax.all_to_all(spectra, "chan", split_axis=1, concat_axis=3, tiled=True),
        "tile",
        split_axis=1,
        concat_axis=2,
        tiled=True,
    )
    spectra_count = turned.shape[3]
    inputs_all = turned.shape[2]
    stacked = stack_operands(turned)
    right_block = jnp.concatenate([turned[0], turned[1]], -1)
    products = pair_products(stacked, right_block) / spectra_count
    row_index = lax.iota(jnp.int32, inputs_all)[:, None]
    col_index = lax.iota(jnp.int32, inputs_all)[None, :]
    packed = jnp.where((col_index >= row_index)[None], products[0], products[1])
    return lax.all_to_all(packed, "tile", split_axis=1, concat_axis=0, tiled=True)


def solution(mesh):
    in_specs = (P("tile", "chan"), P())
    out_specs = P("chan", "tile", None)
    body = per_device if mesh.shape["tile"] == 1 else per_device_tiled
    return jax.shard_map(
        body, mesh=mesh, in_specs=in_specs, out_specs=out_specs, check_vma=False
    )
```

```python
import functools
import math

import jax
import jax.numpy as jnp
import ml_dtypes
import numpy as np
from jax import lax
from jax.experimental import pallas as pl
from jax.experimental.pallas import tpu as pltpu
from jax.sharding import PartitionSpec as P

CHAN = 512
TAPS = 4
VMEM_LIMIT = 56 * 1024 * 1024
FILTER_ROWS = 32
LANES = 128
PITCH = 8


def passed_along(block, axis, distance):
    devices = range(lax.axis_size(axis))
    route = [(i - distance, i) for i in devices if i - distance in devices]
    return lax.ppermute(block, axis, route)


def passed_back_round(block, axis):
    devices = lax.axis_size(axis)
    return lax.ppermute(block, axis, [(i, (i - 1) % devices) for i in range(devices)])


def transform_table(frame_len, channels):
    phase = np.arange(channels)[:, None] * np.arange(frame_len)[None, :] % frame_len
    angle = phase * (2.0 * math.pi / frame_len)
    rows = np.stack([np.cos(angle), -np.sin(angle)], 1) / math.sqrt(frame_len)
    return rows.reshape(2 * channels, frame_len).astype(np.float32).astype(ml_dtypes.bfloat16)


def cost(flops, moved):
    return pl.CostEstimate(flops=flops, bytes_accessed=moved, transcendentals=0)


def filter_transform_kernel(variants, local, dests, splits, sources, *refs):
    follows_ref = refs[0]
    voltage_refs = refs[1 : sources + 1]
    weights_ref, table_ref = refs[sources + 1 : sources + 3]
    out_refs = refs[sources + 3 : -1]
    filtered_ref = refs[-1]
    count, rows, frame_len = filtered_ref.shape

    def filtered_block(spectra, frame_of):
        needed = sorted({s - k for s in spectra for k in range(TAPS)})
        for lane in range(0, frame_len, LANES):
            weights = [
                jnp.broadcast_to(weights_ref[k : k + 1, lane : lane + LANES], (FILTER_ROWS, LANES))
                for k in range(TAPS)
            ]
            kept = [w * follows_ref[0] for w in weights] if max(spectra) >= local else weights

            def body(step, carry, lane=lane, weights=weights, kept=kept):
                at = pl.ds(pl.multiple_of(step * FILTER_ROWS, FILTER_ROWS), FILTER_ROWS)
                frames = {}
                for f in needed:
                    source, place = frame_of[f]
                    start = place * frame_len + lane
                    frames[f] = voltage_refs[source][at, start : start + LANES].astype(jnp.float32)
                for slot, s in enumerate(spectra):
                    total = weights[0] * frames[s]
                    for k in range(1, TAPS):
                        factor = kept[k] if s >= local > s - k else weights[k]
                        total = total + factor * frames[s - k]
                    filtered_ref[slot, at, lane : lane + LANES] = total.astype(jnp.bfloat16)
                return carry

            lax.fori_loop(0, rows // FILTER_ROWS, body, 0, unroll=True)

    for index, variant in enumerate(variants):
        if len(variants) == 1:
            filtered_block(*variant)
        else:
            pl.when(pl.program_id(0) == index)(
                functools.partial(filtered_block, *variant)
            )

    per_dest = table_ref.shape[0] // dests
    dest_block = max(1, min(dests, 256 // per_dest))
    height = dest_block * per_dest
    for slot in range(count):
        filtered = filtered_ref[slot]
        for block in range(dests // dest_block):
            spectrum = lax.dot_general(
                table_ref[block * height : (block + 1) * height, :],
                filtered,
                (((1,), (1,)), ((), ())),
                preferred_element_type=jnp.float32,
            )
            spectrum = spectrum.astype(jnp.bfloat16).reshape(dest_block, per_dest, rows)
            begin = 0
            for out_ref, width in zip(out_refs, splits):
                out_ref[block * dest_block : (block + 1) * dest_block, slot] = spectrum[
                    :, begin : begin + width, :
                ]
                begin += width


def filter_transform(
    arrays, begins, variants, local, follows, weights, table, dests, splits, rows, block, first=0, outs=()
):
    frame_len = table.shape[1]
    count = len(variants[0][0])
    in_specs = [pl.BlockSpec(memory_space=pltpu.SMEM)]
    for a, b in zip(arrays, begins):
        move = 1 if a.shape[0] > block else 0
        in_specs.append(
            pl.BlockSpec((block, a.shape[1]), functools.partial(lambda m, b, i: (i * m + b, 0), move, b))
        )
    in_specs += [
        pl.BlockSpec(weights.shape, lambda i: (0, 0)),
        pl.BlockSpec(table.shape, lambda i: (0, 0)),
    ]
    args = [follows, *arrays, weights, table]
    aliases = {len(args) + i: i for i in range(len(outs))}
    in_specs += [pl.BlockSpec(memory_space=pl.ANY)] * len(outs)
    steps = len(variants) if len(variants) > 1 or len(arrays) > 1 else rows // block

    def kernel(*refs):
        refs = (*refs[: len(args)], *refs[len(args) + len(outs) :])
        filter_transform_kernel(variants, local, dests, tuple(splits), len(arrays), *refs)

    return pl.pallas_call(
        kernel,
        grid=(steps,),
        in_specs=in_specs,
        out_specs=[
            pl.BlockSpec((dests, count, w, block), lambda i: (0, 0, 0, i + first)) for w in splits
        ],
        out_shape=[jax.ShapeDtypeStruct((dests, count, w, rows), jnp.bfloat16) for w in splits],
        scratch_shapes=[pltpu.VMEM((count, block, frame_len), jnp.bfloat16)],
        input_output_aliases=aliases,
        compiler_params=pltpu.CompilerParams(vmem_limit_bytes=VMEM_LIMIT),
        cost_estimate=cost(
            2 * table.size * steps * block * count,
            2 * (sum(a.shape[1] for a in arrays) * steps * block + table.size * (1 + count)),
        ),
        name="filter_transform",
    )(*args, *outs)


def spread(spectra_refs, rolled, scratch):
    base = 0
    tiles = scratch.shape[0]
    for ref, moves in zip(spectra_refs, rolled):
        devices, count, rows, _ = ref.shape
        pitch = rows + PITCH
        for slot in range(count):
            for d in range(devices):
                block = ref[d, slot].astype(jnp.float32)
                for tile in range(tiles):
                    move = moves[slot][tile * len(moves[slot]) // tiles]
                    at = (base + (d + move) % devices) * pitch
                    scratch[tile, at : at + rows, :] = block[:, tile * LANES : (tile + 1) * LANES]
            base += devices


def spread_shape(arrays, lanes):
    depth = sum(a.shape[0] * a.shape[1] for a in arrays)
    return depth, pltpu.VMEM((lanes // LANES, depth * (arrays[0].shape[2] + PITCH), LANES), jnp.float32)


def regroup_kernel(rolled, *refs):
    sources = len(rolled)
    wide_ref, tall_ref, scratch = refs[sources:]
    rows = refs[0].shape[2]
    depth = wide_ref.shape[1] // 2
    spread(refs[:sources], rolled, scratch)
    for channel in range(rows // 2):
        for part in range(2):
            deep = slice(part * depth, (part + 1) * depth)
            for tile in range(scratch.shape[0]):
                across = slice(tile * LANES, (tile + 1) * LANES)
                values = scratch[tile, pl.ds(2 * channel + part, depth, stride=rows + PITCH), :]
                wide_ref[channel, deep, across] = values.astype(jnp.bfloat16)
                tall_ref[channel, across, deep] = values.T.astype(jnp.bfloat16)


def regroup(arrays, rolled, inputs, block):
    rows = arrays[0].shape[2]
    channels = rows // 2
    depth, scratch = spread_shape(arrays, block)
    in_specs = [pl.BlockSpec((*a.shape[:3], block), lambda i: (0, 0, 0, i)) for a in arrays]
    return pl.pallas_call(
        functools.partial(regroup_kernel, rolled),
        grid=(inputs // block,),
        in_specs=in_specs,
        out_specs=[
            pl.BlockSpec((channels, 2 * depth, block), lambda i: (0, 0, i)),
            pl.BlockSpec((channels, block, 2 * depth), lambda i: (0, i, 0)),
        ],
        out_shape=[
            jax.ShapeDtypeStruct((channels, 2 * depth, inputs), jnp.bfloat16),
            jax.ShapeDtypeStruct((channels, inputs, 2 * depth), jnp.bfloat16),
        ],
        scratch_shapes=[scratch],
        compiler_params=pltpu.CompilerParams(vmem_limit_bytes=VMEM_LIMIT),
        cost_estimate=cost(0, 6 * depth * rows * inputs),
        name="regroup",
    )(*arrays)


def packed_square(scale, block, wide, tall, store):
    half = wide.shape[0] // 2
    inputs = wide.shape[1]
    row_index = lax.broadcasted_iota(jnp.int32, (block, block), 0)
    col_index = lax.broadcasted_iota(jnp.int32, (block, block), 1)
    upper = col_index >= row_index
    for first in range(0, inputs, block):
        end = first + block
        re_rows = tall[first:end]
        im_rows = imaginary_rows(re_rows, half)
        im = jnp.dot(im_rows, wide[:, :end], preferred_element_type=jnp.float32) * scale
        re = jnp.dot(re_rows, wide[:, first:], preferred_element_type=jnp.float32) * scale
        if first:
            store(first, 0, im[:, :first])
        store(first, first, jnp.where(upper, re[:, :block], im[:, first:]))
        if end < inputs:
            store(first, end, re[:, block:])


def imaginary_rows(rows, half):
    return jnp.concatenate([rows[:, half:], -rows[:, :half]], 1)


def correlate_first_kernel(scale, block, wide_ref, tall_ref, out_ref):
    for channel in range(out_ref.shape[0]):

        def store(row, col, values, channel=channel):
            height, width = values.shape
            out_ref[channel, row : row + height, col : col + width] = values

        packed_square(scale, block, wide_ref[channel], tall_ref[channel], store)


def correlate_first(wide, tall, block, total, spectra_count):
    channels, depth, inputs = wide.shape
    return pl.pallas_call(
        functools.partial(correlate_first_kernel, 1.0 / spectra_count, block),
        grid=(channels // 2,),
        in_specs=[
            pl.BlockSpec((2, depth, inputs), lambda c: (c, 0, 0)),
            pl.BlockSpec((2, inputs, depth), lambda c: (c, 0, 0)),
        ],
        out_specs=pl.BlockSpec((2, inputs, inputs), lambda c: (c, 0, 0)),
        out_shape=jax.ShapeDtypeStruct((channels, total, total), jnp.float32),
        compiler_params=pltpu.CompilerParams(vmem_limit_bytes=VMEM_LIMIT),
        cost_estimate=cost(
            2 * channels * depth * inputs * inputs, channels * inputs * (4 * depth + 4 * inputs)
        ),
        name="correlate_first",
    )(wide, tall)


def correlate_rest_kernel(scale, block, first_channel, rolled, *refs):
    sources = len(rolled)
    wide_ref, tall_ref = refs[:2]
    spectra_refs = refs[2 : 2 + sources]
    out_ref, scratch, right, below, sems = refs[3 + sources :]
    rows = spectra_refs[0].shape[2]
    depth = wide_ref.shape[1] // 2
    before = wide_ref.shape[2]
    step = pl.program_id(0)
    slot = step % 2

    @pl.when(step == 0)
    def _():
        spread(spectra_refs, rolled, scratch)

    def copies(slot, channel):
        return (
            pltpu.make_async_copy(
                right.at[slot], out_ref.at[channel, pl.ds(0, before), pl.ds(before, right.shape[2])], sems.at[slot, 0]
            ),
            pltpu.make_async_copy(
                below.at[slot], out_ref.at[channel, pl.ds(before, below.shape[1]), :], sems.at[slot, 1]
            ),
        )

    @pl.when(step >= 2)
    def _():
        for copy in copies(slot, first_channel + step - 2):
            copy.wait()

    parts = [
        [
            scratch[tile, pl.ds(2 * step + part, depth, stride=rows + PITCH), :]
            for tile in range(scratch.shape[0])
        ]
        for part in range(2)
    ]
    wide = jnp.concatenate([jnp.concatenate(p, 1) for p in parts], 0).astype(jnp.bfloat16)
    tall = jnp.concatenate([jnp.concatenate([t.T for t in p], 0) for p in parts], 1).astype(jnp.bfloat16)

    right[slot] = jnp.dot(tall_ref[0], wide, preferred_element_type=jnp.float32) * scale
    im_rows = imaginary_rows(tall, depth)
    below[slot, :, :before] = jnp.dot(im_rows, wide_ref[0], preferred_element_type=jnp.float32) * scale

    def store(row, col, values):
        height, width = values.shape
        below[slot, row : row + height, before + col : before + col + width] = values

    packed_square(scale, block, wide, tall, store)
    for copy in copies(slot, first_channel + step):
        copy.start()

    @pl.when(step == pl.num_programs(0) - 1)
    def _():
        for copy in copies(1 - slot, first_channel + step - 1):
            copy.wait()
        for copy in copies(slot, first_channel + step):
            copy.wait()


def correlate_rest(wide, tall, arrays, pieces, rolled, block, first_channel, spectra_count, out):
    _, double, before = wide.shape
    rows, inputs = arrays[-1].shape[2:]
    channels = rows // 2
    shapes = [(*a.shape[:2], rows) for a in arrays]
    in_specs = [
        pl.BlockSpec((1, double, before), lambda c: (c + first_channel, 0, 0)),
        pl.BlockSpec((1, before, double), lambda c: (c + first_channel, 0, 0)),
    ]
    in_specs += [
        pl.BlockSpec((*shape, inputs), functools.partial(lambda p, c: (0, 0, p, 0), p))
        for shape, p in zip(shapes, pieces)
    ]
    in_specs.append(pl.BlockSpec(memory_space=pl.ANY))
    scratch = pltpu.VMEM((inputs // LANES, double // 2 * (rows + PITCH), LANES), jnp.float32)
    return pl.pallas_call(
        functools.partial(correlate_rest_kernel, 1.0 / spectra_count, block, first_channel, rolled),
        grid=(channels,),
        in_specs=in_specs,
        out_specs=pl.BlockSpec(memory_space=pl.ANY),
        out_shape=jax.ShapeDtypeStruct(out.shape, out.dtype),
        scratch_shapes=[
            scratch,
            pltpu.VMEM((2, before, inputs), jnp.float32),
            pltpu.VMEM((2, inputs, before + inputs), jnp.float32),
            pltpu.SemaphoreType.DMA((2, 2)),
        ],
        input_output_aliases={2 + len(arrays): 0},
        compiler_params=pltpu.CompilerParams(vmem_limit_bytes=VMEM_LIMIT),
        cost_estimate=cost(
            2 * channels * double * inputs * (2 * before + inputs),
            channels * inputs * (4 * double + 8 * before + 4 * inputs),
        ),
        name="correlate_rest",
    )(wide, tall, *arrays, out)


def turn(block):
    return lax.all_to_all(block, "chan", split_axis=0, concat_axis=0, tiled=True)


def after(value, earlier):
    return lax.optimization_barrier((value, earlier))[0]


def per_device(voltage, tap_weights):
    frame_len = 2 * CHAN
    inputs, samples = voltage.shape
    local = samples // frame_len
    devices = lax.axis_size("chan")
    channels = CHAN // devices
    count = devices * local
    table = jnp.asarray(transform_table(frame_len, CHAN))
    past = TAPS - 1
    blocks = 4
    block = inputs // blocks
    later = [1, 1, 2, 2]
    follows = jnp.where(lax.axis_index("chan") == devices - 1, 0.0, 1.0).astype(jnp.float32)[None]
    own = {f: (0, f) for f in range(local)}
    inner = [(tuple(range(past, local)), own)]
    groups = [0], [1, 2, 3]
    rolled = [
        (((0,),) * (local - past), ((0,), tuple(int(later[b] == 2) for b in some), (0,)))
        for some in groups
    ]

    def around(voltage, some):
        ahead, back, variants = [], [], []
        for b in some:
            rows = voltage[b * block : (b + 1) * block]
            frame_of = dict(own)
            for f in range(later[b] - past, 0):
                frame_of[f] = (1, len(ahead))
                ahead.append(rows[:, (local + f) * frame_len : (local + f + 1) * frame_len])
            for f in range(later[b]):
                frame_of[local + f] = (2, len(back))
                back.append(rows[:, f * frame_len : (f + 1) * frame_len])
            made = tuple(s + local if s < later[b] else s for s in range(past))
            variants.append((made, frame_of))
        return (jnp.concatenate(ahead, 1), jnp.concatenate(back, 1)), variants

    def neighbours(ahead, back):
        return passed_along(ahead, "chan", 1), passed_back_round(back, "chan")

    def spectra(arrays, begins, variants, splits, rows, *into):
        return filter_transform(
            arrays, begins, variants, local, follows, tap_weights, table, devices, splits, rows, block, *into
        )

    whole, halves = [2 * channels], [channels, channels]
    first_sent, first_variants = around(voltage, groups[0])
    first_around = neighbours(*first_sent)
    second_sent, second_variants = around(after(voltage, first_sent), groups[1])
    second_around = neighbours(*after(second_sent, first_around))
    inner_turned = turn(after(spectra([voltage], [0], inner, whole, inputs)[0], first_around))
    first = spectra([voltage, *first_around], [0, 0, 0], first_variants, whole, block)[0]
    turned = turn(after(first, (inner_turned, second_around)))
    parts = spectra([voltage, *second_around], [1, 0, 0], second_variants, halves, inputs - block)
    wide, tall = regroup([inner_turned, turned], rolled[0], block, block)
    result = correlate_first(wide, tall, block, inputs, count)
    inner_rest = inner_turned[..., block:]
    for piece, part in enumerate(parts):
        turned = turn(after(part, turned))
        result = correlate_rest(
            wide, tall, [inner_rest, turned], [piece, 0], rolled[1], block,
            piece * channels // 2, count, result,
        )
    return result


def stack_operands(turned):
    stacked_re = jnp.concatenate([turned[0], turned[1]], -1)
    stacked_im = jnp.concatenate([turned[1], -turned[0]], -1)
    return jnp.stack([stacked_re, stacked_im], 0)


def pair_products(left_rows, right_cols):
    return jnp.einsum("pcik,cjk->pcij", left_rows, right_cols, preferred_element_type=jnp.float32)


def per_device_tiled(voltage, tap_weights):
    frame_len = 2 * CHAN
    local_inputs, samples = voltage.shape
    spec_local = samples // frame_len
    history_tail = voltage[:, samples - (TAPS - 1) * frame_len :]
    earlier = passed_along(history_tail, "chan", 1)
    extended = jnp.concatenate([earlier, voltage], 1).reshape(
        local_inputs, spec_local + TAPS - 1, frame_len
    )
    filtered = jnp.zeros((local_inputs, spec_local, frame_len), jnp.float32)
    for tap_index in range(TAPS):
        shifted = extended[:, TAPS - 1 - tap_index : TAPS - 1 - tap_index + spec_local, :]
        filtered = filtered + tap_weights[tap_index][None, None, :] * shifted.astype(jnp.float32)
    filtered = filtered.astype(jnp.bfloat16).reshape(local_inputs * spec_local, frame_len)
    dft_table = jnp.asarray(transform_table(frame_len, CHAN)).reshape(CHAN, 2, frame_len)
    dft_table = dft_table.swapaxes(0, 1).reshape(2 * CHAN, frame_len)
    spectra = lax.dot_general(
        dft_table, filtered, (((1,), (1,)), ((), ())), preferred_element_type=jnp.float32
    )
    spectra = spectra.astype(jnp.bfloat16).reshape(2, CHAN, local_inputs, spec_local)
    turned = lax.all_to_all(
        lax.all_to_all(spectra, "chan", split_axis=1, concat_axis=3, tiled=True),
        "tile",
        split_axis=1,
        concat_axis=2,
        tiled=True,
    )
    spectra_count = turned.shape[3]
    inputs_all = turned.shape[2]
    stacked = stack_operands(turned)
    right_block = jnp.concatenate([turned[0], turned[1]], -1)
    products = pair_products(stacked, right_block) / spectra_count
    row_index = lax.iota(jnp.int32, inputs_all)[:, None]
    col_index = lax.iota(jnp.int32, inputs_all)[None, :]
    packed = jnp.where((col_index >= row_index)[None], products[0], products[1])
    return lax.all_to_all(packed, "tile", split_axis=1, concat_axis=0, tiled=True)


def solution(mesh):
    in_specs = (P("tile", "chan"), P())
    out_specs = P("chan", "tile", None)
    body = per_device if mesh.shape["tile"] == 1 else per_device_tiled
    return jax.shard_map(
        body, mesh=mesh, in_specs=in_specs, out_specs=out_specs, check_vma=False
    )
```

```python
import functools
import math

import jax
import jax.numpy as jnp
import ml_dtypes
import numpy as np
from jax import lax
from jax.experimental import pallas as pl
from jax.experimental.pallas import tpu as pltpu
from jax.sharding import PartitionSpec as P

CHAN = 512
TAPS = 4
VMEM_LIMIT = 56 * 1024 * 1024
FILTER_ROWS = 32
LANES = 128
PITCH = 8
PLANE = 8


def passed_along(block, axis, distance):
    devices = range(lax.axis_size(axis))
    route = [(i - distance, i) for i in devices if i - distance in devices]
    return lax.ppermute(block, axis, route)


def passed_back_round(block, axis):
    devices = lax.axis_size(axis)
    return lax.ppermute(block, axis, [(i, (i - 1) % devices) for i in range(devices)])


def transform_table(frame_len, channels):
    phase = np.arange(channels)[:, None] * np.arange(frame_len)[None, :] % frame_len
    angle = phase * (2.0 * math.pi / frame_len)
    rows = np.stack([np.cos(angle), -np.sin(angle)], 1) / math.sqrt(frame_len)
    return rows.reshape(2 * channels, frame_len).astype(np.float32).astype(ml_dtypes.bfloat16)


def cost(flops, moved):
    return pl.CostEstimate(flops=flops, bytes_accessed=moved, transcendentals=0)


def filter_transform_kernel(variants, local, dests, splits, planes, sources, *refs):
    follows_ref, place_ref = refs[:2]
    voltage_refs = refs[2 : sources + 2]
    weights_ref, table_ref = refs[sources + 2 : sources + 4]
    out_refs = refs[sources + 4 : -1]
    filtered_ref = refs[-1]
    count, rows, frame_len = filtered_ref.shape

    def filtered_block(spectra, frame_of):
        needed = sorted({s - k for s in spectra for k in range(TAPS)})
        for lane in range(0, frame_len, LANES):
            weights = [
                jnp.broadcast_to(weights_ref[k : k + 1, lane : lane + LANES], (FILTER_ROWS, LANES))
                for k in range(TAPS)
            ]
            kept = [w * follows_ref[0] for w in weights] if max(spectra) >= local else weights

            def body(step, carry, lane=lane, weights=weights, kept=kept):
                at = pl.ds(pl.multiple_of(step * FILTER_ROWS, FILTER_ROWS), FILTER_ROWS)
                frames = {}
                for f in needed:
                    source, place = frame_of[f]
                    start = place * frame_len + lane
                    frames[f] = voltage_refs[source][at, start : start + LANES].astype(jnp.float32)
                for slot, s in enumerate(spectra):
                    total = weights[0] * frames[s]
                    for k in range(1, TAPS):
                        factor = kept[k] if s >= local > s - k else weights[k]
                        total = total + factor * frames[s - k]
                    filtered_ref[slot, at, lane : lane + LANES] = total.astype(jnp.bfloat16)
                return carry

            lax.fori_loop(0, rows // FILTER_ROWS, body, 0, unroll=True)

    for index, variant in enumerate(variants):
        if len(variants) == 1:
            filtered_block(*variant)
        else:
            pl.when(pl.program_id(0) == index)(
                functools.partial(filtered_block, *variant)
            )

    per_dest = table_ref.shape[0] // dests
    dest_block = dests // planes if planes else max(1, min(dests, 256 // per_dest))
    height = dest_block * per_dest
    for slot in range(count):
        filtered = filtered_ref[slot]
        for block in range(dests // dest_block):
            start = block * height
            if planes:
                start = pl.multiple_of((block ^ place_ref[0]) * height, height)
            spectrum = lax.dot_general(
                table_ref[pl.ds(start, height), :],
                filtered,
                (((1,), (1,)), ((), ())),
                preferred_element_type=jnp.float32,
            )
            spectrum = spectrum.astype(jnp.bfloat16).reshape(dest_block, per_dest, rows)
            if planes:
                for dest in range(dest_block):
                    out_refs[block][dest ^ place_ref[1], slot] = spectrum[dest]
                continue
            begin = 0
            for out_ref, width in zip(out_refs, splits):
                out_ref[block * dest_block : (block + 1) * dest_block, slot] = spectrum[
                    :, begin : begin + width, :
                ]
                begin += width


def filter_transform(
    arrays, begins, variants, local, follows, place, weights, table, dests, splits, planes, rows, block
):
    frame_len = table.shape[1]
    count = len(variants[0][0])
    per_dest = table.shape[0] // dests
    in_specs = [pl.BlockSpec(memory_space=pltpu.SMEM)] * 2
    for source, (a, b) in enumerate(zip(arrays, begins)):
        move = 1 if a.shape[0] > block else 0
        used = [at for _, frame_of in variants for of, at in frame_of.values() if of == source]
        width = (max(used) + 1) * frame_len
        in_specs.append(
            pl.BlockSpec((block, width), functools.partial(lambda m, b, i: (i * m + b, 0), move, b))
        )
    in_specs += [
        pl.BlockSpec(weights.shape, lambda i: (0, 0)),
        pl.BlockSpec(table.shape, lambda i: (0, 0)),
    ]
    if planes:
        shapes = [(dests // planes, count, per_dest)] * planes
    else:
        shapes = [(dests, count, w) for w in splits]
    return pl.pallas_call(
        functools.partial(
            filter_transform_kernel, variants, local, dests, tuple(splits), planes, len(arrays)
        ),
        grid=(rows // block,),
        in_specs=in_specs,
        out_specs=[pl.BlockSpec((*shape, block), lambda i: (0, 0, 0, i)) for shape in shapes],
        out_shape=[jax.ShapeDtypeStruct((*shape, rows), jnp.bfloat16) for shape in shapes],
        scratch_shapes=[pltpu.VMEM((count, block, frame_len), jnp.bfloat16)],
        compiler_params=pltpu.CompilerParams(vmem_limit_bytes=VMEM_LIMIT),
        cost_estimate=cost(
            2 * table.size * rows * count,
            2 * (sum(a.shape[1] for a in arrays) * rows + table.size * (1 + count)),
        ),
        name="filter_transform",
    )(follows, place, *arrays, weights, table)


def spread(spectra_refs, rolled, scratch):
    base = 0
    tiles = scratch.shape[0]
    for ref, moves in zip(spectra_refs, rolled):
        devices, count, rows, _ = ref.shape
        pitch = rows + PITCH
        for slot in range(count):
            for d in range(devices):
                block = ref[d, slot].astype(jnp.float32)
                for tile in range(tiles):
                    move = moves[slot][tile * len(moves[slot]) // tiles]
                    at = (base + (d + move) % devices) * pitch
                    scratch[tile, at : at + rows, :] = block[:, tile * LANES : (tile + 1) * LANES]
            base += devices


def spread_shape(arrays, lanes):
    depth = sum(a.shape[0] * a.shape[1] for a in arrays)
    return depth, pltpu.VMEM((lanes // LANES, depth * (arrays[0].shape[2] + PITCH), LANES), jnp.float32)


def regroup_kernel(rolled, *refs):
    sources = len(rolled)
    wide_ref, tall_ref, scratch = refs[sources:]
    rows = refs[0].shape[2]
    depth = wide_ref.shape[1] // 2
    spread(refs[:sources], rolled, scratch)
    for channel in range(rows // 2):
        for part in range(2):
            deep = slice(part * depth, (part + 1) * depth)
            for tile in range(scratch.shape[0]):
                across = slice(tile * LANES, (tile + 1) * LANES)
                values = scratch[tile, pl.ds(2 * channel + part, depth, stride=rows + PITCH), :]
                wide_ref[channel, deep, across] = values.astype(jnp.bfloat16)
                tall_ref[channel, across, deep] = values.T.astype(jnp.bfloat16)


def regroup(arrays, begins, rolled, inputs, block):
    rows = arrays[0].shape[2]
    channels = rows // 2
    depth, scratch = spread_shape(arrays, block)
    in_specs = [
        pl.BlockSpec((*a.shape[:3], block), functools.partial(lambda b, i: (0, 0, 0, i + b), b))
        for a, b in zip(arrays, begins)
    ]
    return pl.pallas_call(
        functools.partial(regroup_kernel, rolled),
        grid=(inputs // block,),
        in_specs=in_specs,
        out_specs=[
            pl.BlockSpec((channels, 2 * depth, block), lambda i: (0, 0, i)),
            pl.BlockSpec((channels, block, 2 * depth), lambda i: (0, i, 0)),
        ],
        out_shape=[
            jax.ShapeDtypeStruct((channels, 2 * depth, inputs), jnp.bfloat16),
            jax.ShapeDtypeStruct((channels, inputs, 2 * depth), jnp.bfloat16),
        ],
        scratch_shapes=[scratch],
        compiler_params=pltpu.CompilerParams(vmem_limit_bytes=VMEM_LIMIT),
        cost_estimate=cost(0, 6 * depth * rows * inputs),
        name="regroup",
    )(*arrays)


def packed_square(scale, block, wide, tall, store):
    half = wide.shape[0] // 2
    inputs = wide.shape[1]
    row_index = lax.broadcasted_iota(jnp.int32, (block, block), 0)
    col_index = lax.broadcasted_iota(jnp.int32, (block, block), 1)
    upper = col_index >= row_index
    for first in range(0, inputs, block):
        end = first + block
        re_rows = tall[first:end]
        im_rows = imaginary_rows(re_rows, half)
        im = jnp.dot(im_rows, wide[:, :end], preferred_element_type=jnp.float32) * scale
        re = jnp.dot(re_rows, wide[:, first:], preferred_element_type=jnp.float32) * scale
        if first:
            store(first, 0, im[:, :first])
        store(first, first, jnp.where(upper, re[:, :block], im[:, first:]))
        if end < inputs:
            store(first, end, re[:, block:])


def imaginary_rows(rows, half):
    return jnp.concatenate([rows[:, half:], -rows[:, :half]], 1)


def correlate_last_kernel(scale, block, wide_ref, tall_ref, out_ref):
    for channel in range(out_ref.shape[0]):

        def store(row, col, values, channel=channel):
            height, width = values.shape
            out_ref[channel, row : row + height, col : col + width] = values

        packed_square(scale, block, wide_ref[channel], tall_ref[channel], store)


def correlate_last(wide, tall, block, total, spectra_count):
    channels, depth, inputs = wide.shape
    return pl.pallas_call(
        functools.partial(correlate_last_kernel, 1.0 / spectra_count, block),
        grid=(channels // 2,),
        in_specs=[
            pl.BlockSpec((2, depth, inputs), lambda c: (c, 0, 0)),
            pl.BlockSpec((2, inputs, depth), lambda c: (c, 0, 0)),
        ],
        out_specs=pl.BlockSpec((2, inputs, inputs), lambda c: (c, total // inputs - 1, total // inputs - 1)),
        out_shape=jax.ShapeDtypeStruct((channels, total, total), jnp.float32),
        compiler_params=pltpu.CompilerParams(vmem_limit_bytes=VMEM_LIMIT),
        cost_estimate=cost(
            2 * channels * depth * inputs * inputs, channels * inputs * (4 * depth + 4 * inputs)
        ),
        name="correlate_last",
    )(wide, tall)


def correlate_rest_kernel(scale, block, first_channel, rolled, *refs):
    sources = len(rolled)
    wide_ref, tall_ref = refs[:2]
    spectra_refs = refs[2 : 2 + sources]
    out_ref, scratch, above, corner, sems = refs[3 + sources :]
    rows = spectra_refs[0].shape[2]
    depth = wide_ref.shape[1] // 2
    after = wide_ref.shape[2]
    inputs = above.shape[1]
    step = pl.program_id(0)
    slot = step % 2

    @pl.when(step == 0)
    def _():
        spread(spectra_refs, rolled, scratch)

    def copies(slot, channel):
        return (
            pltpu.make_async_copy(
                above.at[slot], out_ref.at[channel, pl.ds(0, inputs), :], sems.at[slot, 0]
            ),
            pltpu.make_async_copy(
                corner.at[slot], out_ref.at[channel, pl.ds(inputs, after), pl.ds(0, inputs)], sems.at[slot, 1]
            ),
        )

    @pl.when(step >= 2)
    def _():
        for copy in copies(slot, first_channel + step - 2):
            copy.wait()

    parts = [
        [
            scratch[tile, pl.ds(2 * step + part, depth, stride=rows + PITCH), :]
            for tile in range(scratch.shape[0])
        ]
        for part in range(2)
    ]
    wide = jnp.concatenate([jnp.concatenate(p, 1) for p in parts], 0).astype(jnp.bfloat16)
    tall = jnp.concatenate([jnp.concatenate([t.T for t in p], 0) for p in parts], 1).astype(jnp.bfloat16)

    above[slot, :, inputs:] = jnp.dot(tall, wide_ref[0], preferred_element_type=jnp.float32) * scale
    im_rows = imaginary_rows(tall_ref[0], depth)
    corner[slot] = jnp.dot(im_rows, wide, preferred_element_type=jnp.float32) * scale

    def store(row, col, values):
        height, width = values.shape
        above[slot, row : row + height, col : col + width] = values

    packed_square(scale, block, wide, tall, store)
    for copy in copies(slot, first_channel + step):
        copy.start()

    @pl.when(step == pl.num_programs(0) - 1)
    def _():
        for copy in copies(1 - slot, first_channel + step - 1):
            copy.wait()
        for copy in copies(slot, first_channel + step):
            copy.wait()


def correlate_rest(wide, tall, arrays, pieces, rolled, block, first_channel, spectra_count, out):
    _, double, last = wide.shape
    rows, inputs = arrays[-1].shape[2:]
    channels = rows // 2
    shapes = [(*a.shape[:2], rows) for a in arrays]
    in_specs = [
        pl.BlockSpec((1, double, last), lambda c: (c + first_channel, 0, 0)),
        pl.BlockSpec((1, last, double), lambda c: (c + first_channel, 0, 0)),
    ]
    in_specs += [
        pl.BlockSpec((*shape, inputs), functools.partial(lambda p, c: (0, 0, p, 0), p))
        for shape, p in zip(shapes, pieces)
    ]
    in_specs.append(pl.BlockSpec(memory_space=pl.ANY))
    scratch = pltpu.VMEM((inputs // LANES, double // 2 * (rows + PITCH), LANES), jnp.float32)
    return pl.pallas_call(
        functools.partial(correlate_rest_kernel, 1.0 / spectra_count, block, first_channel, rolled),
        grid=(channels,),
        in_specs=in_specs,
        out_specs=pl.BlockSpec(memory_space=pl.ANY),
        out_shape=jax.ShapeDtypeStruct(out.shape, out.dtype),
        scratch_shapes=[
            scratch,
            pltpu.VMEM((2, inputs, inputs + last), jnp.float32),
            pltpu.VMEM((2, last, inputs), jnp.float32),
            pltpu.SemaphoreType.DMA((2, 2)),
        ],
        input_output_aliases={2 + len(arrays): 0},
        compiler_params=pltpu.CompilerParams(vmem_limit_bytes=VMEM_LIMIT),
        cost_estimate=cost(
            2 * channels * double * inputs * (2 * last + inputs),
            channels * inputs * (4 * double + 8 * last + 4 * inputs),
        ),
        name="correlate_rest",
    )(wide, tall, *arrays, out)


def turn(block):
    return lax.all_to_all(block, "chan", split_axis=0, concat_axis=0, tiled=True)


def exchanged(block, distance):
    route = [(i, i ^ distance) for i in range(lax.axis_size("chan"))]
    return lax.ppermute(block, "chan", route)


def after(value, earlier):
    return lax.optimization_barrier((value, earlier))[0]


def per_device(voltage, tap_weights):
    frame_len = 2 * CHAN
    inputs, samples = voltage.shape
    local = samples // frame_len
    devices = lax.axis_size("chan")
    channels = CHAN // devices
    count = devices * local
    table = jnp.asarray(transform_table(frame_len, CHAN))
    past = TAPS - 1
    blocks = 4
    block = inputs // blocks
    later = [1, 1, 2, 2]
    me = lax.axis_index("chan")
    follows = jnp.where(me == devices - 1, 0.0, 1.0).astype(jnp.float32)[None]
    place = jnp.stack([me // PLANE, me % PLANE]).astype(jnp.int32)
    own = {f: (0, f) for f in range(local)}
    inner = [(tuple(range(past, local)), own)]
    groups = [3], [0, 1, 2]
    rolled = [
        (((0,),) * (local - past),) * PLANE + (((0,), tuple(int(later[b] == 2) for b in some), (0,)),)
        for some in groups
    ]

    def around(some):
        ahead, back, variants = [], [], []
        for b in some:
            rows = voltage[b * block : (b + 1) * block]
            frame_of = dict(own)
            for f in range(later[b] - past, 0):
                frame_of[f] = (1, len(ahead))
                ahead.append(rows[:, (local + f) * frame_len : (local + f + 1) * frame_len])
            for f in range(later[b]):
                frame_of[local + f] = (2, len(back))
                back.append(rows[:, f * frame_len : (f + 1) * frame_len])
            made = tuple(s + local if s < later[b] else s for s in range(past))
            variants.append((made, frame_of))
        return (jnp.concatenate(ahead, 1), jnp.concatenate(back, 1)), variants

    def neighbours(ahead, back):
        return passed_along(ahead, "chan", 1), passed_back_round(back, "chan")

    def spectra(arrays, begins, variants, splits, rows, planes=0):
        return filter_transform(
            arrays, begins, variants, local, follows, place, tap_weights, table, devices, splits, planes, rows, block
        )

    whole, halves = [2 * channels], [channels, channels]
    sent, variants = around([3, 0, 1, 2])
    arounds = neighbours(*sent)
    inner_blocks = spectra([voltage], [0], inner, whole, inputs, devices // PLANE)
    arrived = [b if k == 0 else exchanged(b, k * PLANE) for k, b in enumerate(inner_blocks)]
    first = spectra([voltage, *arounds], [3, 0, 0], variants[:1], whole, block)[0]
    turned = turn(after(first, arrived))
    stacks = [jnp.concatenate([a[j : j + 1] for a in arrived], 0) for j in range(PLANE)]
    inner_turned = [s if j == 0 else exchanged(s, j) for j, s in enumerate(stacks)]
    parts = spectra([voltage, *arounds], [0, 0, 0], variants[1:], halves, inputs - block)
    wide, tall = regroup([*inner_turned, turned], [3] * PLANE + [0], rolled[0], block, block)
    result = correlate_last(wide, tall, block, inputs, count)
    for piece, part in enumerate(parts):
        turned = turn(after(part, (turned, inner_turned if piece else ())))
        result = correlate_rest(
            wide, tall, [*inner_turned, turned], [piece] * PLANE + [0], rolled[1], block,
            piece * channels // 2, count, result,
        )
    return result


def stack_operands(turned):
    stacked_re = jnp.concatenate([turned[0], turned[1]], -1)
    stacked_im = jnp.concatenate([turned[1], -turned[0]], -1)
    return jnp.stack([stacked_re, stacked_im], 0)


def pair_products(left_rows, right_cols):
    return jnp.einsum("pcik,cjk->pcij", left_rows, right_cols, preferred_element_type=jnp.float32)


def per_device_tiled(voltage, tap_weights):
    frame_len = 2 * CHAN
    local_inputs, samples = voltage.shape
    spec_local = samples // frame_len
    history_tail = voltage[:, samples - (TAPS - 1) * frame_len :]
    earlier = passed_along(history_tail, "chan", 1)
    extended = jnp.concatenate([earlier, voltage], 1).reshape(
        local_inputs, spec_local + TAPS - 1, frame_len
    )
    filtered = jnp.zeros((local_inputs, spec_local, frame_len), jnp.float32)
    for tap_index in range(TAPS):
        shifted = extended[:, TAPS - 1 - tap_index : TAPS - 1 - tap_index + spec_local, :]
        filtered = filtered + tap_weights[tap_index][None, None, :] * shifted.astype(jnp.float32)
    filtered = filtered.astype(jnp.bfloat16).reshape(local_inputs * spec_local, frame_len)
    dft_table = jnp.asarray(transform_table(frame_len, CHAN)).reshape(CHAN, 2, frame_len)
    dft_table = dft_table.swapaxes(0, 1).reshape(2 * CHAN, frame_len)
    spectra = lax.dot_general(
        dft_table, filtered, (((1,), (1,)), ((), ())), preferred_element_type=jnp.float32
    )
    spectra = spectra.astype(jnp.bfloat16).reshape(2, CHAN, local_inputs, spec_local)
    turned = lax.all_to_all(
        lax.all_to_all(spectra, "chan", split_axis=1, concat_axis=3, tiled=True),
        "tile",
        split_axis=1,
        concat_axis=2,
        tiled=True,
    )
    spectra_count = turned.shape[3]
    inputs_all = turned.shape[2]
    stacked = stack_operands(turned)
    right_block = jnp.concatenate([turned[0], turned[1]], -1)
    products = pair_products(stacked, right_block) / spectra_count
    row_index = lax.iota(jnp.int32, inputs_all)[:, None]
    col_index = lax.iota(jnp.int32, inputs_all)[None, :]
    packed = jnp.where((col_index >= row_index)[None], products[0], products[1])
    return lax.all_to_all(packed, "tile", split_axis=1, concat_axis=0, tiled=True)


def solution(mesh):
    in_specs = (P("tile", "chan"), P())
    out_specs = P("chan", "tile", None)
    devices = mesh.shape["chan"]
    planes = devices // PLANE
    fits = devices == planes * PLANE and planes and planes & (planes - 1) == 0
    body = per_device if mesh.shape["tile"] == 1 and fits else per_device_tiled
    return jax.shard_map(
        body, mesh=mesh, in_specs=in_specs, out_specs=out_specs, check_vma=False
    )
```

```python
import functools
import math

import jax
import jax.numpy as jnp
import ml_dtypes
import numpy as np
from jax import lax
from jax.experimental import pallas as pl
from jax.experimental.pallas import tpu as pltpu
from jax.sharding import PartitionSpec as P

CHAN = 512
TAPS = 4
VMEM_LIMIT = 56 * 1024 * 1024
FILTER_ROWS = 32
LANES = 128
PLANE = 8


def passed_along(block, axis, distance):
    devices = range(lax.axis_size(axis))
    route = [(i - distance, i) for i in devices if i - distance in devices]
    return lax.ppermute(block, axis, route)


def passed_back_round(block, axis):
    devices = lax.axis_size(axis)
    return lax.ppermute(block, axis, [(i, (i - 1) % devices) for i in range(devices)])


def transform_table(frame_len, channels):
    phase = np.arange(channels)[:, None] * np.arange(frame_len)[None, :] % frame_len
    angle = phase * (2.0 * math.pi / frame_len)
    rows = np.stack([np.cos(angle), -np.sin(angle)], 1) / math.sqrt(frame_len)
    return rows.reshape(2 * channels, frame_len).astype(np.float32).astype(ml_dtypes.bfloat16)


def cost(flops, moved):
    return pl.CostEstimate(flops=flops, bytes_accessed=moved, transcendentals=0)


def filter_transform_kernel(variants, local, dests, splits, planes, sources, *refs):
    follows_ref, place_ref = refs[:2]
    voltage_refs = refs[2 : sources + 2]
    weights_ref, table_ref = refs[sources + 2 : sources + 4]
    out_refs = refs[sources + 4 : -1]
    filtered_ref = refs[-1]
    count, rows, frame_len = filtered_ref.shape

    def filtered_block(spectra, frame_of):
        needed = sorted({s - k for s in spectra for k in range(TAPS)})
        for lane in range(0, frame_len, LANES):
            weights = [
                jnp.broadcast_to(weights_ref[k : k + 1, lane : lane + LANES], (FILTER_ROWS, LANES))
                for k in range(TAPS)
            ]
            kept = [w * follows_ref[0] for w in weights] if max(spectra) >= local else weights

            def body(step, carry, lane=lane, weights=weights, kept=kept):
                at = pl.ds(pl.multiple_of(step * FILTER_ROWS, FILTER_ROWS), FILTER_ROWS)
                frames = {}
                for f in needed:
                    source, place = frame_of[f]
                    start = place * frame_len + lane
                    frames[f] = voltage_refs[source][at, start : start + LANES].astype(jnp.float32)
                for slot, s in enumerate(spectra):
                    total = weights[0] * frames[s]
                    for k in range(1, TAPS):
                        factor = kept[k] if s >= local > s - k else weights[k]
                        total = total + factor * frames[s - k]
                    filtered_ref[slot, at, lane : lane + LANES] = total.astype(jnp.bfloat16)
                return carry

            lax.fori_loop(0, rows // FILTER_ROWS, body, 0, unroll=True)

    for index, variant in enumerate(variants):
        if len(variants) == 1:
            filtered_block(*variant)
        else:
            pl.when(pl.program_id(0) == index)(
                functools.partial(filtered_block, *variant)
            )

    per_dest = table_ref.shape[0] // dests
    dest_block = dests // planes if planes else max(1, min(dests, 256 // per_dest))
    height = dest_block * per_dest
    for slot in range(count):
        filtered = filtered_ref[slot]
        for block in range(dests // dest_block):
            start = block * height
            if planes:
                start = pl.multiple_of((block ^ place_ref[0]) * height, height)
            spectrum = lax.dot_general(
                table_ref[pl.ds(start, height), :],
                filtered,
                (((1,), (1,)), ((), ())),
                preferred_element_type=jnp.float32,
            )
            spectrum = spectrum.reshape(dest_block, per_dest, rows)
            if planes:
                for dest in range(dest_block):
                    out_refs[block][dest ^ place_ref[1], slot] = spectrum[dest].astype(jnp.bfloat16)
                continue
            begin = 0
            for out_ref, width in zip(out_refs, splits):
                part = spectrum[:, begin : begin + width, :].astype(jnp.bfloat16)
                out_ref[block * dest_block : (block + 1) * dest_block, slot] = part
                begin += width


def filter_transform(
    arrays, begins, variants, local, follows, place, weights, table, dests, splits, planes, rows, block
):
    frame_len = table.shape[1]
    count = len(variants[0][0])
    per_dest = table.shape[0] // dests
    in_specs = [pl.BlockSpec(memory_space=pltpu.SMEM)] * 2
    for source, (a, b) in enumerate(zip(arrays, begins)):
        move = 1 if a.shape[0] > block else 0
        used = [at for _, frame_of in variants for of, at in frame_of.values() if of == source]
        width = (max(used) + 1) * frame_len
        in_specs.append(
            pl.BlockSpec((block, width), functools.partial(lambda m, b, i: (i * m + b, 0), move, b))
        )
    in_specs += [
        pl.BlockSpec(weights.shape, lambda i: (0, 0)),
        pl.BlockSpec(table.shape, lambda i: (0, 0)),
    ]
    if planes:
        shapes = [(dests // planes, count, per_dest)] * planes
    else:
        shapes = [(dests, count, w) for w in splits]
    return pl.pallas_call(
        functools.partial(
            filter_transform_kernel, variants, local, dests, tuple(splits), planes, len(arrays)
        ),
        grid=(rows // block,),
        in_specs=in_specs,
        out_specs=[pl.BlockSpec((*shape, block), lambda i: (0, 0, 0, i)) for shape in shapes],
        out_shape=[jax.ShapeDtypeStruct((*shape, rows), jnp.bfloat16) for shape in shapes],
        scratch_shapes=[pltpu.VMEM((count, block, frame_len), jnp.bfloat16)],
        compiler_params=pltpu.CompilerParams(vmem_limit_bytes=VMEM_LIMIT),
        cost_estimate=cost(
            2 * table.size * rows * count,
            2 * (sum(a.shape[1] for a in arrays) * rows + table.size * (1 + count)),
        ),
        name="filter_transform",
    )(follows, place, *arrays, weights, table)


def pitch_of(rows):
    return (rows // 8 | 1) * 8


def spread(spectra_refs, rolled, scratch):
    base = 0
    tiles = scratch.shape[0]
    for ref, moves in zip(spectra_refs, rolled):
        devices, count, rows, _ = ref.shape
        pitch = pitch_of(rows)
        for slot in range(count):
            for d in range(devices):
                block = ref[d, slot].astype(jnp.float32)
                for tile in range(tiles):
                    move = moves[slot][tile * len(moves[slot]) // tiles]
                    at = (base + (d + move) % devices) * pitch
                    scratch[tile, at : at + rows, :] = block[:, tile * LANES : (tile + 1) * LANES]
            base += devices


def spread_shape(arrays, lanes):
    depth = sum(a.shape[0] * a.shape[1] for a in arrays)
    return depth, pltpu.VMEM((lanes // LANES, depth * pitch_of(arrays[0].shape[2]), LANES), jnp.float32)


def regroup_kernel(rolled, *refs):
    sources = len(rolled)
    wide_ref, tall_ref, scratch = refs[sources:]
    rows = refs[0].shape[2]
    depth = wide_ref.shape[1] // 2
    spread(refs[:sources], rolled, scratch)
    for channel in range(rows // 2):
        for part in range(2):
            deep = slice(part * depth, (part + 1) * depth)
            for tile in range(scratch.shape[0]):
                across = slice(tile * LANES, (tile + 1) * LANES)
                values = scratch[tile, pl.ds(2 * channel + part, depth, stride=pitch_of(rows)), :]
                wide_ref[channel, deep, across] = values.astype(jnp.bfloat16)
                tall_ref[channel, across, deep] = values.T.astype(jnp.bfloat16)


def regroup(arrays, begins, rolled, inputs, block):
    rows = arrays[0].shape[2]
    channels = rows // 2
    depth, scratch = spread_shape(arrays, block)
    in_specs = [
        pl.BlockSpec((*a.shape[:3], block), functools.partial(lambda b, i: (0, 0, 0, i + b), b))
        for a, b in zip(arrays, begins)
    ]
    return pl.pallas_call(
        functools.partial(regroup_kernel, rolled),
        grid=(inputs // block,),
        in_specs=in_specs,
        out_specs=[
            pl.BlockSpec((channels, 2 * depth, block), lambda i: (0, 0, i)),
            pl.BlockSpec((channels, block, 2 * depth), lambda i: (0, i, 0)),
        ],
        out_shape=[
            jax.ShapeDtypeStruct((channels, 2 * depth, inputs), jnp.bfloat16),
            jax.ShapeDtypeStruct((channels, inputs, 2 * depth), jnp.bfloat16),
        ],
        scratch_shapes=[scratch],
        compiler_params=pltpu.CompilerParams(vmem_limit_bytes=VMEM_LIMIT),
        cost_estimate=cost(0, 6 * depth * rows * inputs),
        name="regroup",
    )(*arrays)


def packed_square(scale, block, wide, tall, store):
    half = wide.shape[0] // 2
    inputs = wide.shape[1]
    row_index = lax.broadcasted_iota(jnp.int32, (block, block), 0)
    col_index = lax.broadcasted_iota(jnp.int32, (block, block), 1)
    upper = col_index >= row_index
    for first in range(0, inputs, block):
        end = first + block
        re_rows = tall[first:end]
        im_rows = imaginary_rows(re_rows, half)
        im = jnp.dot(im_rows, wide[:, :end], preferred_element_type=jnp.float32) * scale
        re = jnp.dot(re_rows, wide[:, first:], preferred_element_type=jnp.float32) * scale
        if first:
            store(first, 0, im[:, :first])
        store(first, first, jnp.where(upper, re[:, :block], im[:, first:]))
        if end < inputs:
            store(first, end, re[:, block:])


def imaginary_rows(rows, half):
    return jnp.concatenate([rows[:, half:], -rows[:, :half]], 1)


def correlate_last_kernel(scale, block, wide_ref, tall_ref, out_ref):
    for channel in range(out_ref.shape[0]):

        def store(row, col, values, channel=channel):
            height, width = values.shape
            out_ref[channel, row : row + height, col : col + width] = values

        packed_square(scale, block, wide_ref[channel], tall_ref[channel], store)


def correlate_last(wide, tall, block, total, spectra_count):
    channels, depth, inputs = wide.shape
    return pl.pallas_call(
        functools.partial(correlate_last_kernel, 1.0 / spectra_count, block),
        grid=(channels // 2,),
        in_specs=[
            pl.BlockSpec((2, depth, inputs), lambda c: (c, 0, 0)),
            pl.BlockSpec((2, inputs, depth), lambda c: (c, 0, 0)),
        ],
        out_specs=pl.BlockSpec((2, inputs, inputs), lambda c: (c, total // inputs - 1, total // inputs - 1)),
        out_shape=jax.ShapeDtypeStruct((channels, total, total), jnp.float32),
        compiler_params=pltpu.CompilerParams(vmem_limit_bytes=VMEM_LIMIT),
        cost_estimate=cost(
            2 * channels * depth * inputs * inputs, channels * inputs * (4 * depth + 4 * inputs)
        ),
        name="correlate_last",
    )(wide, tall)


def correlate_rest_kernel(scale, block, first_channel, rolled, *refs):
    sources = len(rolled)
    wide_ref, tall_ref = refs[:2]
    spectra_refs = refs[2 : 2 + sources]
    out_ref, *scratches, above, corner, sems = refs[3 + sources :]
    sets = spectra_refs[:-1], spectra_refs[-1:]
    heights = [refs_of[0].shape[2] for refs_of in sets]
    firsts = first_channel, 0
    depth = wide_ref.shape[1] // 2
    after = wide_ref.shape[2]
    inputs = above.shape[1]
    step = pl.program_id(0)
    slot = step % 2

    @pl.when(step == 0)
    def _():
        spread(sets[0], rolled[:-1], scratches[0])
        spread(sets[1], rolled[-1:], scratches[1])

    def values(tile, part):
        pieces = []
        for scratch, rows, first in zip(scratches, heights, firsts):
            pitch = pitch_of(rows)
            start = 2 * (first + step) + part
            pieces.append(scratch[tile, pl.ds(start, scratch.shape[1] // pitch, stride=pitch), :])
        return jnp.concatenate(pieces, 0)

    def copies(slot, channel):
        return (
            pltpu.make_async_copy(
                above.at[slot], out_ref.at[channel, pl.ds(0, inputs), :], sems.at[slot, 0]
            ),
            pltpu.make_async_copy(
                corner.at[slot], out_ref.at[channel, pl.ds(inputs, after), pl.ds(0, inputs)], sems.at[slot, 1]
            ),
        )

    @pl.when(step >= 2)
    def _():
        for copy in copies(slot, first_channel + step - 2):
            copy.wait()

    parts = [[values(tile, part) for tile in range(scratches[0].shape[0])] for part in range(2)]
    wide = jnp.concatenate([jnp.concatenate(p, 1) for p in parts], 0).astype(jnp.bfloat16)
    tall = jnp.concatenate([jnp.concatenate([t.T for t in p], 0) for p in parts], 1).astype(jnp.bfloat16)

    above[slot, :, inputs:] = jnp.dot(tall, wide_ref[0], preferred_element_type=jnp.float32) * scale
    im_rows = imaginary_rows(tall_ref[0], depth)
    corner[slot] = jnp.dot(im_rows, wide, preferred_element_type=jnp.float32) * scale

    def store(row, col, values):
        height, width = values.shape
        above[slot, row : row + height, col : col + width] = values

    packed_square(scale, block, wide, tall, store)
    for copy in copies(slot, first_channel + step):
        copy.start()

    @pl.when(step == pl.num_programs(0) - 1)
    def _():
        for copy in copies(1 - slot, first_channel + step - 1):
            copy.wait()
        for copy in copies(slot, first_channel + step):
            copy.wait()


def correlate_rest(wide, tall, arrays, rolled, block, first_channel, spectra_count, out):
    _, double, last = wide.shape
    rows, inputs = arrays[-1].shape[2:]
    channels = rows // 2
    in_specs = [
        pl.BlockSpec((1, double, last), lambda c: (c + first_channel, 0, 0)),
        pl.BlockSpec((1, last, double), lambda c: (c + first_channel, 0, 0)),
    ]
    in_specs += [pl.BlockSpec((*a.shape[:3], inputs), lambda c: (0, 0, 0, 0)) for a in arrays]
    in_specs.append(pl.BlockSpec(memory_space=pl.ANY))
    scratches = [spread_shape(some, inputs)[1] for some in (arrays[:-1], arrays[-1:])]
    return pl.pallas_call(
        functools.partial(correlate_rest_kernel, 1.0 / spectra_count, block, first_channel, rolled),
        grid=(channels,),
        in_specs=in_specs,
        out_specs=pl.BlockSpec(memory_space=pl.ANY),
        out_shape=jax.ShapeDtypeStruct(out.shape, out.dtype),
        scratch_shapes=[
            *scratches,
            pltpu.VMEM((2, inputs, inputs + last), jnp.float32),
            pltpu.VMEM((2, last, inputs), jnp.float32),
            pltpu.SemaphoreType.DMA((2, 2)),
        ],
        input_output_aliases={2 + len(arrays): 0},
        compiler_params=pltpu.CompilerParams(vmem_limit_bytes=VMEM_LIMIT),
        cost_estimate=cost(
            2 * channels * double * inputs * (2 * last + inputs),
            channels * inputs * (4 * double + 8 * last + 4 * inputs),
        ),
        name="correlate_rest",
    )(wide, tall, *arrays, out)


def turn(block):
    return lax.all_to_all(block, "chan", split_axis=0, concat_axis=0, tiled=True)


def exchanged(block, distance):
    route = [(i, i ^ distance) for i in range(lax.axis_size("chan"))]
    return lax.ppermute(block, "chan", route)


def after(value, earlier):
    return lax.optimization_barrier((value, earlier))[0]


def per_device(voltage, tap_weights):
    frame_len = 2 * CHAN
    inputs, samples = voltage.shape
    local = samples // frame_len
    devices = lax.axis_size("chan")
    channels = CHAN // devices
    count = devices * local
    table = jnp.asarray(transform_table(frame_len, CHAN))
    past = TAPS - 1
    blocks = 4
    block = inputs // blocks
    later = [1, 1, 2, 2]
    me = lax.axis_index("chan")
    follows = jnp.where(me == devices - 1, 0.0, 1.0).astype(jnp.float32)[None]
    place = jnp.stack([me // PLANE, me % PLANE]).astype(jnp.int32)
    own = {f: (0, f) for f in range(local)}
    inner = [(tuple(range(past, local)), own)]
    groups = [3], [0, 1, 2]
    rolled = [
        (((0,),) * (local - past),) * PLANE + (((0,), tuple(int(later[b] == 2) for b in some), (0,)),)
        for some in groups
    ]

    def around(some):
        ahead, back, variants = [], [], []
        for b in some:
            rows = voltage[b * block : (b + 1) * block]
            frame_of = dict(own)
            for f in range(later[b] - past, 0):
                frame_of[f] = (1, len(ahead))
                ahead.append(rows[:, (local + f) * frame_len : (local + f + 1) * frame_len])
            for f in range(later[b]):
                frame_of[local + f] = (2, len(back))
                back.append(rows[:, f * frame_len : (f + 1) * frame_len])
            made = tuple(s + local if s < later[b] else s for s in range(past))
            variants.append((made, frame_of))
        return (jnp.concatenate(ahead, 1), jnp.concatenate(back, 1)), variants

    def neighbours(ahead, back):
        return passed_along(ahead, "chan", 1), passed_back_round(back, "chan")

    def spectra(arrays, begins, variants, splits, rows, planes=0):
        return filter_transform(
            arrays, begins, variants, local, follows, place, tap_weights, table, devices, splits, planes, rows, block
        )

    whole = [2 * channels]
    shares = [channels - channels // 4, channels // 4]
    sent, variants = around([3, 0, 1, 2])
    arounds = neighbours(*sent)
    inner_blocks = spectra([voltage], [0], inner, whole, inputs, devices // PLANE)
    arrived = [b if k == 0 else exchanged(b, k * PLANE) for k, b in enumerate(inner_blocks)]
    first = spectra([voltage, *arounds], [3, 0, 0], variants[:1], whole, block)[0]
    turned = turn(after(first, arrived))
    stacks = [jnp.concatenate([a[j : j + 1] for a in arrived], 0) for j in range(PLANE)]
    inner_turned = [s if j == 0 else exchanged(s, j) for j, s in enumerate(stacks)]
    parts = spectra([voltage, *arounds], [0, 0, 0], variants[1:], [2 * c for c in shares], inputs - block)
    wide, tall = regroup([*inner_turned, turned], [3] * PLANE + [0], rolled[0], block, block)
    result = correlate_last(wide, tall, block, inputs, count)
    first_turned = turn(after(parts[0], turned))
    part, result, first_turned = lax.optimization_barrier((parts[1], result, first_turned))
    second_turned = turn(part)
    begin = 0
    for share, turned in zip(shares, (first_turned, second_turned)):
        result = correlate_rest(
            wide, tall, [*inner_turned, turned], rolled[1], block, begin, count, result
        )
        begin += share
    return result


def stack_operands(turned):
    stacked_re = jnp.concatenate([turned[0], turned[1]], -1)
    stacked_im = jnp.concatenate([turned[1], -turned[0]], -1)
    return jnp.stack([stacked_re, stacked_im], 0)


def pair_products(left_rows, right_cols):
    return jnp.einsum("pcik,cjk->pcij", left_rows, right_cols, preferred_element_type=jnp.float32)


def per_device_tiled(voltage, tap_weights):
    frame_len = 2 * CHAN
    local_inputs, samples = voltage.shape
    spec_local = samples // frame_len
    history_tail = voltage[:, samples - (TAPS - 1) * frame_len :]
    earlier = passed_along(history_tail, "chan", 1)
    extended = jnp.concatenate([earlier, voltage], 1).reshape(
        local_inputs, spec_local + TAPS - 1, frame_len
    )
    filtered = jnp.zeros((local_inputs, spec_local, frame_len), jnp.float32)
    for tap_index in range(TAPS):
        shifted = extended[:, TAPS - 1 - tap_index : TAPS - 1 - tap_index + spec_local, :]
        filtered = filtered + tap_weights[tap_index][None, None, :] * shifted.astype(jnp.float32)
    filtered = filtered.astype(jnp.bfloat16).reshape(local_inputs * spec_local, frame_len)
    dft_table = jnp.asarray(transform_table(frame_len, CHAN)).reshape(CHAN, 2, frame_len)
    dft_table = dft_table.swapaxes(0, 1).reshape(2 * CHAN, frame_len)
    spectra = lax.dot_general(
        dft_table, filtered, (((1,), (1,)), ((), ())), preferred_element_type=jnp.float32
    )
    spectra = spectra.astype(jnp.bfloat16).reshape(2, CHAN, local_inputs, spec_local)
    turned = lax.all_to_all(
        lax.all_to_all(spectra, "chan", split_axis=1, concat_axis=3, tiled=True),
        "tile",
        split_axis=1,
        concat_axis=2,
        tiled=True,
    )
    spectra_count = turned.shape[3]
    inputs_all = turned.shape[2]
    stacked = stack_operands(turned)
    right_block = jnp.concatenate([turned[0], turned[1]], -1)
    products = pair_products(stacked, right_block) / spectra_count
    row_index = lax.iota(jnp.int32, inputs_all)[:, None]
    col_index = lax.iota(jnp.int32, inputs_all)[None, :]
    packed = jnp.where((col_index >= row_index)[None], products[0], products[1])
    return lax.all_to_all(packed, "tile", split_axis=1, concat_axis=0, tiled=True)


def solution(mesh):
    in_specs = (P("tile", "chan"), P())
    out_specs = P("chan", "tile", None)
    devices = mesh.shape["chan"]
    planes = devices // PLANE
    fits = devices == planes * PLANE and planes and planes & (planes - 1) == 0
    body = per_device if mesh.shape["tile"] == 1 and fits else per_device_tiled
    return jax.shard_map(
        body, mesh=mesh, in_specs=in_specs, out_specs=out_specs, check_vma=False
    )
```

```python
import functools
import math

import jax
import jax.numpy as jnp
import ml_dtypes
import numpy as np
from jax import lax
from jax.experimental import pallas as pl
from jax.experimental.pallas import tpu as pltpu
from jax.sharding import PartitionSpec as P

CHAN = 512
TAPS = 4
VMEM_LIMIT = 56 * 1024 * 1024
FILTER_ROWS = 32
LANES = 128
PLANE = 8


def passed_along(block, axis, distance):
    devices = range(lax.axis_size(axis))
    route = [(i - distance, i) for i in devices if i - distance in devices]
    return lax.ppermute(block, axis, route)


def passed_back_round(block, axis):
    devices = lax.axis_size(axis)
    return lax.ppermute(block, axis, [(i, (i - 1) % devices) for i in range(devices)])


def transform_table(frame_len, channels):
    phase = np.arange(channels)[:, None] * np.arange(frame_len)[None, :] % frame_len
    angle = phase * (2.0 * math.pi / frame_len)
    rows = np.stack([np.cos(angle), -np.sin(angle)], 1) / math.sqrt(frame_len)
    return rows.reshape(2 * channels, frame_len).astype(np.float32).astype(ml_dtypes.bfloat16)


def cost(flops, moved):
    return pl.CostEstimate(flops=flops, bytes_accessed=moved, transcendentals=0)


def filter_transform_kernel(variants, local, dests, splits, planes, sources, *refs):
    follows_ref, place_ref = refs[:2]
    voltage_refs = refs[2 : sources + 2]
    weights_ref, table_ref = refs[sources + 2 : sources + 4]
    out_refs = refs[sources + 4 : -1]
    filtered_ref = refs[-1]
    count, rows, frame_len = filtered_ref.shape

    def filtered_block(spectra, frame_of):
        needed = sorted({s - k for s in spectra for k in range(TAPS)})
        for lane in range(0, frame_len, LANES):
            weights = [
                jnp.broadcast_to(weights_ref[k : k + 1, lane : lane + LANES], (FILTER_ROWS, LANES))
                for k in range(TAPS)
            ]
            kept = [w * follows_ref[0] for w in weights] if max(spectra) >= local else weights

            def body(step, carry, lane=lane, weights=weights, kept=kept):
                at = pl.ds(pl.multiple_of(step * FILTER_ROWS, FILTER_ROWS), FILTER_ROWS)
                frames = {}
                for f in needed:
                    source, place = frame_of[f]
                    start = place * frame_len + lane
                    frames[f] = voltage_refs[source][at, start : start + LANES].astype(jnp.float32)
                for slot, s in enumerate(spectra):
                    total = weights[0] * frames[s]
                    for k in range(1, TAPS):
                        factor = kept[k] if s >= local > s - k else weights[k]
                        total = total + factor * frames[s - k]
                    filtered_ref[slot, at, lane : lane + LANES] = total.astype(jnp.bfloat16)
                return carry

            lax.fori_loop(0, rows // FILTER_ROWS, body, 0, unroll=True)

    for index, variant in enumerate(variants):
        if len(variants) == 1:
            filtered_block(*variant)
        else:
            pl.when(pl.program_id(0) == index)(
                functools.partial(filtered_block, *variant)
            )

    per_dest = table_ref.shape[0] // dests
    dest_block = dests // planes if planes else max(1, min(dests, 256 // per_dest))
    height = dest_block * per_dest
    for slot in range(count):
        filtered = filtered_ref[slot]
        for block in range(dests // dest_block):
            start = block * height
            if planes:
                start = pl.multiple_of((block ^ place_ref[0]) * height, height)
            spectrum = lax.dot_general(
                table_ref[pl.ds(start, height), :],
                filtered,
                (((1,), (1,)), ((), ())),
                preferred_element_type=jnp.float32,
            )
            spectrum = spectrum.reshape(dest_block, per_dest, rows)
            if planes:
                for dest in range(dest_block):
                    out_refs[block][dest ^ place_ref[1], slot] = spectrum[dest].astype(jnp.bfloat16)
                continue
            begin = 0
            for out_ref, width in zip(out_refs, splits):
                part = spectrum[:, begin : begin + width, :].astype(jnp.bfloat16)
                out_ref[block * dest_block : (block + 1) * dest_block, slot] = part
                begin += width


def filter_transform(
    arrays, begins, variants, local, follows, place, weights, table, dests, splits, planes, rows, block
):
    frame_len = table.shape[1]
    count = len(variants[0][0])
    per_dest = table.shape[0] // dests
    in_specs = [pl.BlockSpec(memory_space=pltpu.SMEM)] * 2
    for source, (a, b) in enumerate(zip(arrays, begins)):
        move = 1 if a.shape[0] > block else 0
        used = [at for _, frame_of in variants for of, at in frame_of.values() if of == source]
        width = (max(used) + 1) * frame_len
        in_specs.append(
            pl.BlockSpec((block, width), functools.partial(lambda m, b, i: (i * m + b, 0), move, b))
        )
    in_specs += [
        pl.BlockSpec(weights.shape, lambda i: (0, 0)),
        pl.BlockSpec(table.shape, lambda i: (0, 0)),
    ]
    if planes:
        shapes = [(dests // planes, count, per_dest)] * planes
    else:
        shapes = [(dests, count, w) for w in splits]
    return pl.pallas_call(
        functools.partial(
            filter_transform_kernel, variants, local, dests, tuple(splits), planes, len(arrays)
        ),
        grid=(rows // block,),
        in_specs=in_specs,
        out_specs=[pl.BlockSpec((*shape, block), lambda i: (0, 0, 0, i)) for shape in shapes],
        out_shape=[jax.ShapeDtypeStruct((*shape, rows), jnp.bfloat16) for shape in shapes],
        scratch_shapes=[pltpu.VMEM((count, block, frame_len), jnp.bfloat16)],
        compiler_params=pltpu.CompilerParams(vmem_limit_bytes=VMEM_LIMIT),
        cost_estimate=cost(
            2 * table.size * rows * count,
            2 * (sum(a.shape[1] for a in arrays) * rows + table.size * (1 + count)),
        ),
        name="filter_transform",
    )(follows, place, *arrays, weights, table)


def pitch_of(rows):
    return (rows // 8 | 1) * 8


def spread(spectra_refs, rolled, scratch):
    base = 0
    tiles = scratch.shape[0]
    for ref, moves in zip(spectra_refs, rolled):
        devices, count, rows, _ = ref.shape
        pitch = pitch_of(rows)
        for slot in range(count):
            for d in range(devices):
                block = ref[d, slot].astype(jnp.float32)
                for tile in range(tiles):
                    move = moves[slot][tile * len(moves[slot]) // tiles]
                    at = (base + (d + move) % devices) * pitch
                    scratch[tile, at : at + rows, :] = block[:, tile * LANES : (tile + 1) * LANES]
            base += devices


def spread_shape(arrays, lanes):
    depth = sum(a.shape[0] * a.shape[1] for a in arrays)
    return depth, pltpu.VMEM((lanes // LANES, depth * pitch_of(arrays[0].shape[2]), LANES), jnp.float32)


def packed_square(scale, block, wide, tall, store):
    half = wide.shape[0] // 2
    inputs = wide.shape[1]
    row_index = lax.broadcasted_iota(jnp.int32, (block, block), 0)
    col_index = lax.broadcasted_iota(jnp.int32, (block, block), 1)
    upper = col_index >= row_index
    for first in range(0, inputs, block):
        end = first + block
        re_rows = tall[first:end]
        im_rows = imaginary_rows(re_rows, half)
        im = jnp.dot(im_rows, wide[:, :end], preferred_element_type=jnp.float32) * scale
        re = jnp.dot(re_rows, wide[:, first:], preferred_element_type=jnp.float32) * scale
        if first:
            store(first, 0, im[:, :first])
        store(first, first, jnp.where(upper, re[:, :block], im[:, first:]))
        if end < inputs:
            store(first, end, re[:, block:])


def imaginary_rows(rows, half):
    return jnp.concatenate([rows[:, half:], -rows[:, :half]], 1)


def correlate_kernel(scale, block, first_channel, rolled, *refs):
    sources = len(rolled)
    sets = refs[: sources - 1], refs[sources - 1 : sources]
    out_ref, *scratches, square, sems = refs[-5:]
    heights = [refs_of[0].shape[2] for refs_of in sets]
    firsts = first_channel, 0
    step = pl.program_id(0)
    slot = step % 2

    @pl.when(step == 0)
    def _():
        spread(sets[0], rolled[:-1], scratches[0])
        spread(sets[1], rolled[-1:], scratches[1])

    def values(tile, part):
        pieces = []
        for scratch, rows, first in zip(scratches, heights, firsts):
            pitch = pitch_of(rows)
            start = 2 * (first + step) + part
            pieces.append(scratch[tile, pl.ds(start, scratch.shape[1] // pitch, stride=pitch), :])
        return jnp.concatenate(pieces, 0)

    def copy(slot, step):
        return pltpu.make_async_copy(square.at[slot], out_ref.at[first_channel + step], sems.at[slot])

    @pl.when(step >= 2)
    def _():
        copy(slot, step - 2).wait()

    parts = [[values(tile, part) for tile in range(scratches[0].shape[0])] for part in range(2)]
    wide = jnp.concatenate([jnp.concatenate(p, 1) for p in parts], 0).astype(jnp.bfloat16)
    tall = jnp.concatenate([jnp.concatenate([t.T for t in p], 0) for p in parts], 1).astype(jnp.bfloat16)

    def store(row, col, values):
        height, width = values.shape
        square[slot, row : row + height, col : col + width] = values

    packed_square(scale, block, wide, tall, store)
    copy(slot, step).start()

    @pl.when(step == pl.num_programs(0) - 1)
    def _():
        copy(1 - slot, step - 1).wait()
        copy(slot, step).wait()


def correlate(arrays, rolled, block, total_channels, first_channel, spectra_count, out=None):
    rows, inputs = arrays[-1].shape[2:]
    channels = rows // 2
    in_specs = [pl.BlockSpec(a.shape, lambda c: (0, 0, 0, 0)) for a in arrays]
    args, aliases = list(arrays), {}
    if out is not None:
        in_specs.append(pl.BlockSpec(memory_space=pl.ANY))
        aliases = {len(args): 0}
        args.append(out)
    scratches, depths = [], 0
    for some in (arrays[:-1], arrays[-1:]):
        depth, scratch = spread_shape(some, inputs)
        scratches.append(scratch)
        depths += depth
    return pl.pallas_call(
        functools.partial(correlate_kernel, 1.0 / spectra_count, block, first_channel, rolled),
        grid=(channels,),
        in_specs=in_specs,
        out_specs=pl.BlockSpec(memory_space=pl.ANY),
        out_shape=jax.ShapeDtypeStruct((total_channels, inputs, inputs), jnp.float32),
        scratch_shapes=[
            *scratches,
            pltpu.VMEM((2, inputs, inputs), jnp.float32),
            pltpu.SemaphoreType.DMA((2,)),
        ],
        input_output_aliases=aliases,
        compiler_params=pltpu.CompilerParams(vmem_limit_bytes=VMEM_LIMIT),
        cost_estimate=cost(
            4 * channels * depths * inputs * inputs, channels * inputs * (4 * depths + 4 * inputs)
        ),
        name="correlate",
    )(*args)


def turn(block):
    return lax.all_to_all(block, "chan", split_axis=0, concat_axis=0, tiled=True)


def exchanged(block, distance):
    route = [(i, i ^ distance) for i in range(lax.axis_size("chan"))]
    return lax.ppermute(block, "chan", route)


def after(value, earlier):
    return lax.optimization_barrier((value, earlier))[0]


def per_device(voltage, tap_weights):
    frame_len = 2 * CHAN
    inputs, samples = voltage.shape
    local = samples // frame_len
    devices = lax.axis_size("chan")
    channels = CHAN // devices
    count = devices * local
    table = jnp.asarray(transform_table(frame_len, CHAN))
    past = TAPS - 1
    blocks = 4
    block = inputs // blocks
    later = [1, 1, 2, 2]
    me = lax.axis_index("chan")
    follows = jnp.where(me == devices - 1, 0.0, 1.0).astype(jnp.float32)[None]
    place = jnp.stack([me // PLANE, me % PLANE]).astype(jnp.int32)
    own = {f: (0, f) for f in range(local)}
    inner = [(tuple(range(past, local)), own)]
    rolled = (((0,),) * (local - past),) * PLANE + (((0,), tuple(int(b == 2) for b in later), (0,)),)

    def around(some):
        ahead, back, variants = [], [], []
        for b in some:
            rows = voltage[b * block : (b + 1) * block]
            frame_of = dict(own)
            for f in range(later[b] - past, 0):
                frame_of[f] = (1, len(ahead))
                ahead.append(rows[:, (local + f) * frame_len : (local + f + 1) * frame_len])
            for f in range(later[b]):
                frame_of[local + f] = (2, len(back))
                back.append(rows[:, f * frame_len : (f + 1) * frame_len])
            made = tuple(s + local if s < later[b] else s for s in range(past))
            variants.append((made, frame_of))
        return (jnp.concatenate(ahead, 1), jnp.concatenate(back, 1)), variants

    def neighbours(ahead, back):
        return passed_along(ahead, "chan", 1), passed_back_round(back, "chan")

    def spectra(arrays, begins, variants, splits, rows, planes=0):
        return filter_transform(
            arrays, begins, variants, local, follows, place, tap_weights, table, devices, splits, planes, rows, block
        )

    shares = [channels - channels // 4, channels // 4]
    sent, variants = around(range(blocks))
    arounds = neighbours(*sent)
    inner_blocks = spectra([voltage], [0], inner, [2 * channels], inputs, devices // PLANE)
    arrived = [b if k == 0 else exchanged(b, k * PLANE) for k, b in enumerate(inner_blocks)]
    parts = spectra([voltage, *arounds], [0, 0, 0], variants, [2 * c for c in shares], inputs)
    first_turned = turn(after(parts[0], arrived))
    stacks = [jnp.concatenate([a[j : j + 1] for a in arrived], 0) for j in range(PLANE)]
    inner_turned = [s if j == 0 else exchanged(s, j) for j, s in enumerate(stacks)]
    second_turned = turn(after(parts[1], (first_turned, inner_turned)))
    result, begin = None, 0
    for share, turned in zip(shares, (first_turned, second_turned)):
        result = correlate([*inner_turned, turned], rolled, block, channels, begin, count, result)
        begin += share
    return result


def stack_operands(turned):
    stacked_re = jnp.concatenate([turned[0], turned[1]], -1)
    stacked_im = jnp.concatenate([turned[1], -turned[0]], -1)
    return jnp.stack([stacked_re, stacked_im], 0)


def pair_products(left_rows, right_cols):
    return jnp.einsum("pcik,cjk->pcij", left_rows, right_cols, preferred_element_type=jnp.float32)


def per_device_tiled(voltage, tap_weights):
    frame_len = 2 * CHAN
    local_inputs, samples = voltage.shape
    spec_local = samples // frame_len
    history_tail = voltage[:, samples - (TAPS - 1) * frame_len :]
    earlier = passed_along(history_tail, "chan", 1)
    extended = jnp.concatenate([earlier, voltage], 1).reshape(
        local_inputs, spec_local + TAPS - 1, frame_len
    )
    filtered = jnp.zeros((local_inputs, spec_local, frame_len), jnp.float32)
    for tap_index in range(TAPS):
        shifted = extended[:, TAPS - 1 - tap_index : TAPS - 1 - tap_index + spec_local, :]
        filtered = filtered + tap_weights[tap_index][None, None, :] * shifted.astype(jnp.float32)
    filtered = filtered.astype(jnp.bfloat16).reshape(local_inputs * spec_local, frame_len)
    dft_table = jnp.asarray(transform_table(frame_len, CHAN)).reshape(CHAN, 2, frame_len)
    dft_table = dft_table.swapaxes(0, 1).reshape(2 * CHAN, frame_len)
    spectra = lax.dot_general(
        dft_table, filtered, (((1,), (1,)), ((), ())), preferred_element_type=jnp.float32
    )
    spectra = spectra.astype(jnp.bfloat16).reshape(2, CHAN, local_inputs, spec_local)
    turned = lax.all_to_all(
        lax.all_to_all(spectra, "chan", split_axis=1, concat_axis=3, tiled=True),
        "tile",
        split_axis=1,
        concat_axis=2,
        tiled=True,
    )
    spectra_count = turned.shape[3]
    inputs_all = turned.shape[2]
    stacked = stack_operands(turned)
    right_block = jnp.concatenate([turned[0], turned[1]], -1)
    products = pair_products(stacked, right_block) / spectra_count
    row_index = lax.iota(jnp.int32, inputs_all)[:, None]
    col_index = lax.iota(jnp.int32, inputs_all)[None, :]
    packed = jnp.where((col_index >= row_index)[None], products[0], products[1])
    return lax.all_to_all(packed, "tile", split_axis=1, concat_axis=0, tiled=True)


def solution(mesh):
    in_specs = (P("tile", "chan"), P())
    out_specs = P("chan", "tile", None)
    devices = mesh.shape["chan"]
    planes = devices // PLANE
    fits = devices == planes * PLANE and planes and planes & (planes - 1) == 0 and CHAN // devices % 16 == 0
    body = per_device if mesh.shape["tile"] == 1 and fits else per_device_tiled
    return jax.shard_map(
        body, mesh=mesh, in_specs=in_specs, out_specs=out_specs, check_vma=False
    )
```

```python
import functools
import math

import jax
import jax.numpy as jnp
import ml_dtypes
import numpy as np
from jax import lax
from jax.experimental import pallas as pl
from jax.experimental.pallas import tpu as pltpu
from jax.sharding import PartitionSpec as P

CHAN = 512
TAPS = 4
VMEM_LIMIT = 56 * 1024 * 1024
FILTER_ROWS = 32
LANES = 128
PLANE = 8


def passed_along(block, axis, distance):
    devices = range(lax.axis_size(axis))
    route = [(i - distance, i) for i in devices if i - distance in devices]
    return lax.ppermute(block, axis, route)


def passed_back_round(block, axis):
    devices = lax.axis_size(axis)
    return lax.ppermute(block, axis, [(i, (i - 1) % devices) for i in range(devices)])


def transform_table(frame_len, channels):
    phase = np.arange(channels)[:, None] * np.arange(frame_len)[None, :] % frame_len
    angle = phase * (2.0 * math.pi / frame_len)
    rows = np.stack([np.cos(angle), -np.sin(angle)], 1) / math.sqrt(frame_len)
    return rows.reshape(2 * channels, frame_len).astype(np.float32).astype(ml_dtypes.bfloat16)


def cost(flops, moved):
    return pl.CostEstimate(flops=flops, bytes_accessed=moved, transcendentals=0)


def filter_transform_kernel(variants, local, dests, splits, planes, sources, *refs):
    follows_ref, place_ref = refs[:2]
    voltage_refs = refs[2 : sources + 2]
    weights_ref, table_ref = refs[sources + 2 : sources + 4]
    out_refs = refs[sources + 4 : -1]
    filtered_ref = refs[-1]
    count, rows, frame_len = filtered_ref.shape

    def filtered_block(spectra, frame_of):
        needed = sorted({s - k for s in spectra for k in range(TAPS)})
        for lane in range(0, frame_len, LANES):
            weights = [
                jnp.broadcast_to(weights_ref[k : k + 1, lane : lane + LANES], (FILTER_ROWS, LANES))
                for k in range(TAPS)
            ]
            kept = [w * follows_ref[0] for w in weights] if max(spectra) >= local else weights

            def body(step, carry, lane=lane, weights=weights, kept=kept):
                at = pl.ds(pl.multiple_of(step * FILTER_ROWS, FILTER_ROWS), FILTER_ROWS)
                frames = {}
                for f in needed:
                    source, place = frame_of[f]
                    start = place * frame_len + lane
                    frames[f] = voltage_refs[source][at, start : start + LANES].astype(jnp.float32)
                for slot, s in enumerate(spectra):
                    total = weights[0] * frames[s]
                    for k in range(1, TAPS):
                        factor = kept[k] if s >= local > s - k else weights[k]
                        total = total + factor * frames[s - k]
                    filtered_ref[slot, at, lane : lane + LANES] = total.astype(jnp.bfloat16)
                return carry

            lax.fori_loop(0, rows // FILTER_ROWS, body, 0, unroll=True)

    for index, variant in enumerate(variants):
        if len(variants) == 1:
            filtered_block(*variant)
        else:
            pl.when(pl.program_id(0) == index)(
                functools.partial(filtered_block, *variant)
            )

    per_dest = table_ref.shape[0] // dests
    dest_block = dests // planes if planes else min(dests, 1 << (256 // per_dest).bit_length() - 1)
    height = dest_block * per_dest
    for slot in range(count):
        filtered = filtered_ref[slot]
        for block in range(dests // dest_block):
            start = block * height
            if planes:
                start = pl.multiple_of((block ^ place_ref[0]) * height, height)
            spectrum = lax.dot_general(
                table_ref[pl.ds(start, height), :],
                filtered,
                (((1,), (1,)), ((), ())),
                preferred_element_type=jnp.float32,
            )
            spectrum = spectrum.reshape(dest_block, per_dest, rows)
            if planes:
                for dest in range(dest_block):
                    out_refs[block][dest ^ place_ref[1], slot] = spectrum[dest].astype(jnp.bfloat16)
                continue
            begin = 0
            for out_ref, width in zip(out_refs, splits):
                part = spectrum[:, begin : begin + width, :].astype(jnp.bfloat16)
                out_ref[block * dest_block : (block + 1) * dest_block, slot] = part
                begin += width


def filter_transform(
    arrays, begins, variants, local, follows, place, weights, table, dests, splits, planes, rows, block
):
    frame_len = table.shape[1]
    count = len(variants[0][0])
    per_dest = table.shape[0] // dests
    in_specs = [pl.BlockSpec(memory_space=pltpu.SMEM)] * 2
    for source, (a, b) in enumerate(zip(arrays, begins)):
        move = 1 if a.shape[0] > block else 0
        used = [at for _, frame_of in variants for of, at in frame_of.values() if of == source]
        width = (max(used) + 1) * frame_len
        in_specs.append(
            pl.BlockSpec((block, width), functools.partial(lambda m, b, i: (i * m + b, 0), move, b))
        )
    in_specs += [
        pl.BlockSpec(weights.shape, lambda i: (0, 0)),
        pl.BlockSpec(table.shape, lambda i: (0, 0)),
    ]
    if planes:
        shapes = [(dests // planes, count, per_dest)] * planes
    else:
        shapes = [(dests, count, w) for w in splits]
    return pl.pallas_call(
        functools.partial(
            filter_transform_kernel, variants, local, dests, tuple(splits), planes, len(arrays)
        ),
        grid=(rows // block,),
        in_specs=in_specs,
        out_specs=[pl.BlockSpec((*shape, block), lambda i: (0, 0, 0, i)) for shape in shapes],
        out_shape=[jax.ShapeDtypeStruct((*shape, rows), jnp.bfloat16) for shape in shapes],
        scratch_shapes=[pltpu.VMEM((count, block, frame_len), jnp.bfloat16)],
        compiler_params=pltpu.CompilerParams(vmem_limit_bytes=VMEM_LIMIT),
        cost_estimate=cost(
            2 * table.size * rows * count,
            2 * (sum(a.shape[1] for a in arrays) * rows + table.size * (1 + count)),
        ),
        name="filter_transform",
    )(follows, place, *arrays, weights, table)


def pitch_of(rows):
    return (rows // 8 | 1) * 8


def spread(spectra_refs, rolled, scratch):
    base = 0
    tiles = scratch.shape[0]
    for ref, moves in zip(spectra_refs, rolled):
        devices, count, rows, _ = ref.shape
        pitch = pitch_of(rows)
        for slot in range(count):
            for d in range(devices):
                block = ref[d, slot].astype(jnp.float32)
                for tile in range(tiles):
                    move = moves[slot][tile * len(moves[slot]) // tiles]
                    at = (base + (d + move) % devices) * pitch
                    scratch[tile, at : at + rows, :] = block[:, tile * LANES : (tile + 1) * LANES]
            base += devices


def spread_shape(arrays, lanes):
    depth = sum(a.shape[0] * a.shape[1] for a in arrays)
    return depth, pltpu.VMEM((lanes // LANES, depth * pitch_of(arrays[0].shape[2]), LANES), jnp.float32)


def packed_square(scale, block, wide, tall, store):
    half = wide.shape[0] // 2
    inputs = wide.shape[1]
    row_index = lax.broadcasted_iota(jnp.int32, (block, block), 0)
    col_index = lax.broadcasted_iota(jnp.int32, (block, block), 1)
    upper = col_index >= row_index
    for first in range(0, inputs, block):
        end = first + block
        re_rows = tall[first:end]
        im_rows = imaginary_rows(re_rows, half)
        im = jnp.dot(im_rows, wide[:, :end], preferred_element_type=jnp.float32) * scale
        re = jnp.dot(re_rows, wide[:, first:], preferred_element_type=jnp.float32) * scale
        if first:
            store(first, 0, im[:, :first])
        store(first, first, jnp.where(upper, re[:, :block], im[:, first:]))
        if end < inputs:
            store(first, end, re[:, block:])


def imaginary_rows(rows, half):
    return jnp.concatenate([rows[:, half:], -rows[:, :half]], 1)


def correlate_kernel(scale, block, first_channel, rolled, *refs):
    sources = len(rolled)
    sets = refs[: sources - 1], refs[sources - 1 : sources]
    out_ref, *scratches, square, sems = refs[-5:]
    heights = [refs_of[0].shape[2] for refs_of in sets]
    firsts = first_channel, 0
    step = pl.program_id(0)
    slot = step % 2

    @pl.when(step == 0)
    def _():
        spread(sets[0], rolled[:-1], scratches[0])
        spread(sets[1], rolled[-1:], scratches[1])

    def values(tile, part):
        pieces = []
        for scratch, rows, first in zip(scratches, heights, firsts):
            pitch = pitch_of(rows)
            start = 2 * (first + step) + part
            pieces.append(scratch[tile, pl.ds(start, scratch.shape[1] // pitch, stride=pitch), :])
        return jnp.concatenate(pieces, 0)

    def copy(slot, step):
        return pltpu.make_async_copy(square.at[slot], out_ref.at[first_channel + step], sems.at[slot])

    @pl.when(step >= 2)
    def _():
        copy(slot, step - 2).wait()

    parts = [[values(tile, part) for tile in range(scratches[0].shape[0])] for part in range(2)]
    wide = jnp.concatenate([jnp.concatenate(p, 1) for p in parts], 0).astype(jnp.bfloat16)
    tall = jnp.concatenate([jnp.concatenate([t.T for t in p], 0) for p in parts], 1).astype(jnp.bfloat16)

    def store(row, col, values):
        height, width = values.shape
        square[slot, row : row + height, col : col + width] = values

    packed_square(scale, block, wide, tall, store)
    copy(slot, step).start()

    @pl.when(step == pl.num_programs(0) - 1)
    def _():
        copy(1 - slot, step - 1).wait()
        copy(slot, step).wait()


def correlate(arrays, rolled, block, total_channels, first_channel, spectra_count, out=None):
    rows, inputs = arrays[-1].shape[2:]
    channels = rows // 2
    in_specs = [pl.BlockSpec(a.shape, lambda c: (0, 0, 0, 0)) for a in arrays]
    args, aliases = list(arrays), {}
    if out is not None:
        in_specs.append(pl.BlockSpec(memory_space=pl.ANY))
        aliases = {len(args): 0}
        args.append(out)
    scratches, depths = [], 0
    for some in (arrays[:-1], arrays[-1:]):
        depth, scratch = spread_shape(some, inputs)
        scratches.append(scratch)
        depths += depth
    return pl.pallas_call(
        functools.partial(correlate_kernel, 1.0 / spectra_count, block, first_channel, rolled),
        grid=(channels,),
        in_specs=in_specs,
        out_specs=pl.BlockSpec(memory_space=pl.ANY),
        out_shape=jax.ShapeDtypeStruct((total_channels, inputs, inputs), jnp.float32),
        scratch_shapes=[
            *scratches,
            pltpu.VMEM((2, inputs, inputs), jnp.float32),
            pltpu.SemaphoreType.DMA((2,)),
        ],
        input_output_aliases=aliases,
        compiler_params=pltpu.CompilerParams(vmem_limit_bytes=VMEM_LIMIT),
        cost_estimate=cost(
            4 * channels * depths * inputs * inputs, channels * inputs * (4 * depths + 4 * inputs)
        ),
        name="correlate",
    )(*args)


def turn(block):
    return lax.all_to_all(block, "chan", split_axis=0, concat_axis=0, tiled=True)


def exchanged(block, distance):
    route = [(i, i ^ distance) for i in range(lax.axis_size("chan"))]
    return lax.ppermute(block, "chan", route)


def after(value, earlier):
    return lax.optimization_barrier((value, earlier))[0]


def per_device(voltage, tap_weights):
    frame_len = 2 * CHAN
    inputs, samples = voltage.shape
    local = samples // frame_len
    devices = lax.axis_size("chan")
    channels = CHAN // devices
    count = devices * local
    table = transform_table(frame_len, CHAN)
    past = TAPS - 1
    blocks = 4
    block = inputs // blocks
    later = [1, 1, 2, 2]
    me = lax.axis_index("chan")
    follows = jnp.where(me == devices - 1, 0.0, 1.0).astype(jnp.float32)[None]
    place = jnp.stack([me // PLANE, me % PLANE]).astype(jnp.int32)
    own = {f: (0, f) for f in range(local)}
    inner = [(tuple(range(past, local)), own)]
    rolled = (((0,),) * (local - past),) * PLANE + (((0,), tuple(int(b == 2) for b in later), (0,)),)

    def around(some):
        ahead, back, variants = [], [], []
        for b in some:
            rows = voltage[b * block : (b + 1) * block]
            frame_of = dict(own)
            for f in range(later[b] - past, 0):
                frame_of[f] = (1, len(ahead))
                ahead.append(rows[:, (local + f) * frame_len : (local + f + 1) * frame_len])
            for f in range(later[b]):
                frame_of[local + f] = (2, len(back))
                back.append(rows[:, f * frame_len : (f + 1) * frame_len])
            made = tuple(s + local if s < later[b] else s for s in range(past))
            variants.append((made, frame_of))
        return (jnp.concatenate(ahead, 1), jnp.concatenate(back, 1)), variants

    def neighbours(ahead, back):
        return passed_along(ahead, "chan", 1), passed_back_round(back, "chan")

    def spectra(arrays, begins, variants, table, rows, planes=0):
        return filter_transform(
            arrays, begins, variants, local, follows, place, tap_weights, jnp.asarray(table), devices, [table.shape[0] // devices], planes, rows, block
        )

    shares = [channels - channels // 4, channels // 4]
    sent, variants = around(range(blocks))
    arounds = neighbours(*sent)
    inner_blocks = spectra([voltage], [0], inner, table, inputs, devices // PLANE)
    arrived = [b if k == 0 else exchanged(b, k * PLANE) for k, b in enumerate(inner_blocks)]
    by_device = table.reshape(devices, 2 * channels, frame_len)
    parts = []
    for own in np.split(by_device, [2 * shares[0]], 1):
        parts += spectra([voltage, *arounds], [0, 0, 0], variants, own.reshape(-1, frame_len), inputs)
    first_turned = turn(after(parts[0], arrived))
    stacks = [jnp.concatenate([a[j : j + 1] for a in arrived], 0) for j in range(PLANE)]
    inner_turned = [s if j == 0 else exchanged(s, j) for j, s in enumerate(stacks)]
    second_turned = turn(after(parts[1], (first_turned, inner_turned)))
    result, begin = None, 0
    for share, turned in zip(shares, (first_turned, second_turned)):
        result = correlate([*inner_turned, turned], rolled, block, channels, begin, count, result)
        begin += share
    return result


def stack_operands(turned):
    stacked_re = jnp.concatenate([turned[0], turned[1]], -1)
    stacked_im = jnp.concatenate([turned[1], -turned[0]], -1)
    return jnp.stack([stacked_re, stacked_im], 0)


def pair_products(left_rows, right_cols):
    return jnp.einsum("pcik,cjk->pcij", left_rows, right_cols, preferred_element_type=jnp.float32)


def per_device_tiled(voltage, tap_weights):
    frame_len = 2 * CHAN
    local_inputs, samples = voltage.shape
    spec_local = samples // frame_len
    history_tail = voltage[:, samples - (TAPS - 1) * frame_len :]
    earlier = passed_along(history_tail, "chan", 1)
    extended = jnp.concatenate([earlier, voltage], 1).reshape(
        local_inputs, spec_local + TAPS - 1, frame_len
    )
    filtered = jnp.zeros((local_inputs, spec_local, frame_len), jnp.float32)
    for tap_index in range(TAPS):
        shifted = extended[:, TAPS - 1 - tap_index : TAPS - 1 - tap_index + spec_local, :]
        filtered = filtered + tap_weights[tap_index][None, None, :] * shifted.astype(jnp.float32)
    filtered = filtered.astype(jnp.bfloat16).reshape(local_inputs * spec_local, frame_len)
    dft_table = jnp.asarray(transform_table(frame_len, CHAN)).reshape(CHAN, 2, frame_len)
    dft_table = dft_table.swapaxes(0, 1).reshape(2 * CHAN, frame_len)
    spectra = lax.dot_general(
        dft_table, filtered, (((1,), (1,)), ((), ())), preferred_element_type=jnp.float32
    )
    spectra = spectra.astype(jnp.bfloat16).reshape(2, CHAN, local_inputs, spec_local)
    turned = lax.all_to_all(
        lax.all_to_all(spectra, "chan", split_axis=1, concat_axis=3, tiled=True),
        "tile",
        split_axis=1,
        concat_axis=2,
        tiled=True,
    )
    spectra_count = turned.shape[3]
    inputs_all = turned.shape[2]
    stacked = stack_operands(turned)
    right_block = jnp.concatenate([turned[0], turned[1]], -1)
    products = pair_products(stacked, right_block) / spectra_count
    row_index = lax.iota(jnp.int32, inputs_all)[:, None]
    col_index = lax.iota(jnp.int32, inputs_all)[None, :]
    packed = jnp.where((col_index >= row_index)[None], products[0], products[1])
    return lax.all_to_all(packed, "tile", split_axis=1, concat_axis=0, tiled=True)


def solution(mesh):
    in_specs = (P("tile", "chan"), P())
    out_specs = P("chan", "tile", None)
    devices = mesh.shape["chan"]
    planes = devices // PLANE
    fits = devices == planes * PLANE and planes and planes & (planes - 1) == 0 and CHAN // devices % 16 == 0
    body = per_device if mesh.shape["tile"] == 1 and fits else per_device_tiled
    return jax.shard_map(
        body, mesh=mesh, in_specs=in_specs, out_specs=out_specs, check_vma=False
    )
```
